32 devices in a mesh: dp: 2 (over core), seq: 16 (over z, y, x).
Axes of the slice: x: 2, y: 2, z: 4, core: 2. Of those that a mesh axis runs over, the one named last changes fastest.
Arguments:
- value_branch: bfloat16 [512, 4096], P(None, ('dp', 'seq')), parts along dimension 1, may hold values from -6 to 6
- first_gate: bfloat16 [512, 4096], P(None, ('dp', 'seq')), parts along dimension 1, may hold values from -6 to 6
- second_gate: bfloat16 [512, 4096], P(None, ('dp', 'seq')), parts along dimension 1, may hold values from -6 to 6
- out_cotangent: bfloat16 [512, 4096], P(None, ('dp', 'seq')), parts along dimension 1, may hold values from -6 to 6
- pos_weight: float32 [64, 33], replicated, may hold values from -4 to 4
- pos_bias: float32 [64], replicated, may hold values from -3.140625 to 3.140625
- mid_weight: float32 [64, 64], replicated, may hold values from -0.75 to 0.75
- mid_bias: float32 [64], replicated, may hold values from -3.140625 to 3.140625
- out_weight: float32 [1024, 64], replicated, may hold values from -0.046875 to 0.046875
- decay_rates: float32 [1024], replicated, may hold values from 3.07 to 15.35
Outputs:
- value_grad: bfloat16 [512, 4096], P(None, ('dp', 'seq')), parts along dimension 1
- first_gate_grad: bfloat16 [512, 4096], P(None, ('dp', 'seq')), parts along dimension 1
- second_gate_grad: bfloat16 [512, 4096], P(None, ('dp', 'seq')), parts along dimension 1
- pos_weight_grad: float32 [128, 33], P('dp'), parts along dimension 0
- pos_bias_grad: float32 [128], P('dp'), parts along dimension 0
- mid_weight_grad: float32 [128, 64], P('dp'), parts along dimension 0
- mid_bias_grad: float32 [128], P('dp'), parts along dimension 0
- out_weight_grad: float32 [1024, 128], P('seq', 'dp'), parts along dimension 1
The draws below stay inside these ranges and needn't reach their ends.
There are 2 independent parts, one for each index of `dp`. The reference program is written for one: setup_inputs(seed, part) draws one part's arguments, and reference() takes and returns one part's arrays. A program takes and returns all parts, laid end to end along the dimension named above; an argument that names none is the same for every part. Nothing has to cross between parts.
All inputs are finite; a program needn't handle non-finite values.
Results may differ from the reference program's by a relative error of at most 0.017.
Values may be sent and summed in bfloat16 or wider, within the bound.
A program may use at most 64 MiB of HBM per device.

```python
import math
import jax
import jax.numpy as jnp
from jax import lax

D = 512
FILTER_WIDTH = 64
BANDS = 16
RADIX = 128
PE_FEATURES = 33
SEQLEN = 2048
FREQ_ROWS = 32


def levels(own_key, shape, split, least, high):
    gain, own = 1.0, jax.random.fold_in(own_key, 6)
    for axis_at, parts in split:
        steps = jnp.exp(jax.random.uniform(jax.random.fold_in(own, axis_at), (parts,), jnp.float32, least / len(split), high / len(split)))
        gain = gain * jnp.repeat(steps, shape[axis_at] // parts).reshape([-1 if axis == axis_at else 1 for axis in range(len(shape))])
    return gain


def bell_draw(own_key, dims, scale, most, split=(), kind=jnp.bfloat16):
    loudness = levels(own_key, dims, split, -0.22, 0.18) if split else 1.0
    result = jax.random.normal(own_key, dims, jnp.float32) * scale * loudness
    return jnp.minimum(jnp.maximum(result, -most), most).astype(kind)


def setup_inputs(seed: int = 0, part: int = 0) -> dict:
    splits = jax.random.split(jax.random.key(seed), 11)
    part_keys = jax.random.split(jax.random.fold_in(splits[10], part), 11)
    return {
        "value_branch": bell_draw(part_keys[0], (D, SEQLEN), 1.0, 6.0, ((1, 16),)),
        "first_gate": bell_draw(part_keys[1], (D, SEQLEN), 1.0, 6.0, ((1, 16),)),
        "second_gate": bell_draw(part_keys[2], (D, SEQLEN), 1.0, 6.0, ((1, 16),)),
        "out_cotangent": bell_draw(part_keys[3], (D, SEQLEN), 1.0, 6.0, ((1, 16),)),
        "pos_weight": bell_draw(splits[4], (FILTER_WIDTH, PE_FEATURES), 1.0, 4.0, (), jnp.float32),
        "pos_bias": jnp.clip(jax.random.uniform(splits[5], (FILTER_WIDTH,), jnp.float32, -3.140625, 3.140625), -3.140625, 3.140625),
        "mid_weight": bell_draw(splits[6], (FILTER_WIDTH, FILTER_WIDTH), FILTER_WIDTH ** -0.5, 0.75, (), jnp.float32),
        "mid_bias": jnp.clip(jax.random.uniform(splits[7], (FILTER_WIDTH,), jnp.float32, -3.140625, 3.140625), -3.140625, 3.140625),
        "out_weight": bell_draw(splits[8], (2 * D, FILTER_WIDTH), (FILTER_WIDTH * SEQLEN // 8) ** -0.5, 0.046875, (), jnp.float32),
        "decay_rates": jnp.clip(jnp.exp(jax.random.uniform(splits[9], (2 * D,), jnp.float32, math.log(3.07), math.log(15.35))), 3.07, 15.35),
    }


def rounded(value):
    return lax.optimization_barrier(value.astype(jnp.bfloat16)).astype(jnp.float32)


def make_tables(freq_rows, radix):
    length_all = freq_rows * radix
    freq_index = jnp.arange(freq_rows, dtype=jnp.int32)
    half_index = jnp.arange(freq_rows // 2, dtype=jnp.int32)
    inner_index = jnp.arange(radix, dtype=jnp.int32)
    angle_one = ((freq_index[:, None] * half_index[None, :]) % freq_rows).astype(jnp.float32) * (2.0 * math.pi / freq_rows)
    angle_two = ((inner_index[:, None] * inner_index[None, :]) % radix).astype(jnp.float32) * (2.0 * math.pi / radix)
    angle_twid = ((freq_index[:, None] * inner_index[None, :]) % length_all).astype(jnp.float32) * (2.0 * math.pi / length_all)
    return (rounded(jnp.cos(angle_one)), rounded(jnp.sin(angle_one)), rounded(jnp.cos(angle_two)),
            rounded(jnp.sin(angle_two)), jnp.cos(angle_twid), jnp.sin(angle_twid))


def section_left(table, data):
    return jnp.einsum("kn,rnm->rkm", table, data, precision=lax.Precision.HIGHEST)


def section_right(data, table):
    return jnp.einsum("rkn,nm->rkm", data, table, precision=lax.Precision.HIGHEST)


def final_section(table, data):
    return jnp.einsum("kn,rkm->rnm", table, data, precision=lax.Precision.HIGHEST)


def forward_spectrum(signal, tables, freq_rows, radix):
    cos_one, sin_one, cos_two, sin_two, twid_cos, twid_sin = tables
    count = signal.shape[0]
    shaped = signal.astype(jnp.float32).reshape(count, freq_rows // 2, radix)
    real_a = section_left(cos_one, shaped)
    imag_a = -section_left(sin_one, shaped)
    real_b = rounded(real_a * twid_cos + imag_a * twid_sin)
    imag_b = rounded(imag_a * twid_cos - real_a * twid_sin)
    real_x = section_right(real_b, cos_two) + section_right(imag_b, sin_two)
    imag_x = section_right(imag_b, cos_two) - section_right(real_b, sin_two)
    return real_x, imag_x


def inverse_signal(product, tables, freq_rows, radix):
    cos_one, sin_one, cos_two, sin_two, twid_cos, twid_sin = tables
    real_p, imag_p = product
    real_q = section_right(real_p, cos_two) - section_right(imag_p, sin_two)
    imag_q = section_right(imag_p, cos_two) + section_right(real_p, sin_two)
    real_r = rounded(real_q * twid_cos - imag_q * twid_sin)
    imag_r = rounded(imag_q * twid_cos + real_q * twid_sin)
    output = final_section(cos_one, real_r) - final_section(sin_one, imag_r)
    count = real_p.shape[0]
    return (output * (1.0 / (freq_rows * radix))).reshape(count, freq_rows // 2 * radix)


def spectral_product(left, right, conj_left, conj_right):
    sign_left = -1.0 if conj_left else 1.0
    sign_right = -1.0 if conj_right else 1.0
    real_part = left[0] * right[0] - sign_left * sign_right * left[1] * right[1]
    imag_part = sign_left * left[1] * right[0] + sign_right * left[0] * right[1]
    return rounded(real_part), rounded(imag_part)


def channel_block(value_blk, first_blk, second_blk, cot_blk, filt_blk, tables, freq_rows, radix):
    count = value_blk.shape[0]
    seq_len = value_blk.shape[1]
    filt_real, filt_imag = forward_spectrum(filt_blk, tables, freq_rows, radix)
    filt_real = filt_real.reshape(count, 2, freq_rows, radix)
    filt_imag = filt_imag.reshape(count, 2, freq_rows, radix)
    spec_one = (filt_real[:, 0], filt_imag[:, 0])
    spec_two = (filt_real[:, 1], filt_imag[:, 1])
    spec_val = forward_spectrum(value_blk, tables, freq_rows, radix)
    conv_one = inverse_signal(spectral_product(spec_one, spec_val, False, False), tables, freq_rows, radix)
    gated = rounded(first_blk.astype(jnp.float32) * conv_one)
    spec_gated = forward_spectrum(gated, tables, freq_rows, radix)
    conv_two = inverse_signal(spectral_product(spec_two, spec_gated, False, False), tables, freq_rows, radix)
    cot_wide = cot_blk.astype(jnp.float32)
    second_grad = (cot_wide * conv_two).astype(jnp.bfloat16)
    grad_two = rounded(cot_wide * second_blk.astype(jnp.float32))
    spec_gtwo = forward_spectrum(grad_two, tables, freq_rows, radix)
    gated_grad = inverse_signal(spectral_product(spec_two, spec_gtwo, True, False), tables, freq_rows, radix)
    filt_grad_two = inverse_signal(spectral_product(spec_gtwo, spec_gated, False, True), tables, freq_rows, radix)
    first_grad = (gated_grad * conv_one).astype(jnp.bfloat16)
    grad_one = rounded(gated_grad * first_blk.astype(jnp.float32))
    spec_gone = forward_spectrum(grad_one, tables, freq_rows, radix)
    value_grad = inverse_signal(spectral_product(spec_one, spec_gone, True, False), tables, freq_rows, radix).astype(jnp.bfloat16)
    filt_grad_one = inverse_signal(spectral_product(spec_gone, spec_val, False, True), tables, freq_rows, radix)
    filt_grads = jnp.stack([filt_grad_one, filt_grad_two], axis=1).reshape(2 * count, seq_len)
    return value_grad, first_grad, second_grad, filt_grads


def positional_features(positions, seq_len, bands):
    band_index = jnp.arange(1, bands + 1, dtype=jnp.int32)
    angles = ((band_index[:, None] * positions[None, :]) % seq_len).astype(jnp.float32) * (2.0 * math.pi / seq_len)
    ramp = positions.astype(jnp.float32)[None, :] / seq_len
    return jnp.concatenate([ramp, jnp.cos(angles), jnp.sin(angles)], axis=0)


def contract_last(left, right):
    return lax.dot_general(left, right, (((1,), (1,)), ((), ())), precision=lax.Precision.HIGHEST)


def reference(value_branch, first_gate, second_gate, out_cotangent, pos_weight, pos_bias, mid_weight, mid_bias, out_weight, decay_rates):
    positions = jnp.arange(SEQLEN, dtype=jnp.int32)
    features = positional_features(positions, SEQLEN, BANDS)
    pre_one = jnp.dot(pos_weight, features, precision=lax.Precision.HIGHEST) + pos_bias[:, None]
    act_one = jnp.sin(pre_one)
    pre_two = jnp.dot(mid_weight, act_one, precision=lax.Precision.HIGHEST) + mid_bias[:, None]
    act_two = jnp.sin(pre_two)
    window = jnp.exp(-decay_rates[:, None] * positions.astype(jnp.float32)[None, :] / SEQLEN)
    filters = (jnp.dot(out_weight, act_two, precision=lax.Precision.HIGHEST) * window).astype(jnp.bfloat16)
    tables = make_tables(FREQ_ROWS, RADIX)
    group_size = 16
    blocks = D // group_size

    def run_block(items):
        return channel_block(items[0], items[1], items[2], items[3], items[4], tables, FREQ_ROWS, RADIX)

    results = lax.map(run_block, (value_branch.reshape(blocks, group_size, SEQLEN),
                                  first_gate.reshape(blocks, group_size, SEQLEN),
                                  second_gate.reshape(blocks, group_size, SEQLEN),
                                  out_cotangent.reshape(blocks, group_size, SEQLEN),
                                  filters.reshape(blocks, 2 * group_size, SEQLEN)))
    value_grad = results[0].reshape(D, SEQLEN)
    first_gate_grad = results[1].reshape(D, SEQLEN)
    second_gate_grad = results[2].reshape(D, SEQLEN)
    filter_grad = results[3].reshape(2 * D, SEQLEN) * window / SEQLEN
    out_weight_grad = contract_last(filter_grad, act_two)
    pre_two_grad = jnp.dot(out_weight.T, filter_grad, precision=lax.Precision.HIGHEST) * jnp.cos(pre_two)
    mid_weight_grad = contract_last(pre_two_grad, act_one)
    mid_bias_grad = jnp.sum(pre_two_grad, axis=1)
    pre_one_grad = jnp.dot(mid_weight.T, pre_two_grad, precision=lax.Precision.HIGHEST) * jnp.cos(pre_one)
    pos_weight_grad = contract_last(pre_one_grad, features)
    pos_bias_grad = jnp.sum(pre_one_grad, axis=1)
    return (value_grad, first_gate_grad, second_gate_grad, pos_weight_grad, pos_bias_grad,
            mid_weight_grad, mid_bias_grad, out_weight_grad)
```

```python
import functools
import math

import jax
import jax.numpy as jnp
import ml_dtypes
import numpy as np
from jax import lax
from jax.experimental import pallas as pl
from jax.experimental.pallas import tpu as pltpu
from jax.sharding import PartitionSpec as P

RADIX = 128
GROUP = 16
MESH = pl.DeviceIdType.MESH
HIGHEST = lax.Precision.HIGHEST


def make_tables(freq_rows, radix):
    length_all = freq_rows * radix
    freq_index = jnp.arange(freq_rows, dtype=jnp.int32)
    half_index = jnp.arange(freq_rows // 2, dtype=jnp.int32)
    inner_index = jnp.arange(radix, dtype=jnp.int32)
    angle_one = (freq_index[:, None] * half_index[None, :] % freq_rows).astype(jnp.float32) * (
        2.0 * math.pi / freq_rows
    )
    angle_two = (inner_index[:, None] * inner_index[None, :] % radix).astype(jnp.float32) * (
        2.0 * math.pi / radix
    )
    angle_twid = (freq_index[:, None] * inner_index[None, :] % length_all).astype(jnp.float32) * (
        2.0 * math.pi / length_all
    )
    cos_one = jnp.cos(angle_one).astype(jnp.bfloat16)
    sin_one = jnp.sin(angle_one).astype(jnp.bfloat16)
    cos_two = jnp.cos(angle_two).astype(jnp.bfloat16)
    sin_two = jnp.sin(angle_two).astype(jnp.bfloat16)
    left_table = jnp.concatenate([cos_one, -sin_one], axis=0)
    right_fwd = jnp.concatenate(
        [jnp.concatenate([cos_two, -sin_two], axis=1), jnp.concatenate([sin_two, cos_two], axis=1)],
        axis=0,
    )
    right_inv = jnp.concatenate(
        [jnp.concatenate([cos_two, sin_two], axis=1), jnp.concatenate([-sin_two, cos_two], axis=1)],
        axis=0,
    )
    return (left_table, right_fwd, right_inv, jnp.cos(angle_twid), jnp.sin(angle_twid))


def forward_spectrum(signal, tables, freq_rows, radix):
    left_table, right_fwd, right_inv, twid_cos, twid_sin = tables
    count = signal.shape[0]
    shaped = signal.reshape(count, freq_rows // 2, radix)
    stacked = jnp.einsum("kn,rnm->rkm", left_table, shaped, preferred_element_type=jnp.float32)
    real_a = stacked[:, :freq_rows]
    imag_a = stacked[:, freq_rows:]
    real_b = (real_a * twid_cos + imag_a * twid_sin).astype(jnp.bfloat16)
    imag_b = (imag_a * twid_cos - real_a * twid_sin).astype(jnp.bfloat16)
    joined = jnp.concatenate([real_b, imag_b], axis=2)
    spectrum = jnp.einsum("rkn,nm->rkm", joined, right_fwd, preferred_element_type=jnp.float32)
    return (spectrum[:, :, :radix], spectrum[:, :, radix:])


def inverse_signal(product, tables, freq_rows, radix):
    left_table, right_fwd, right_inv, twid_cos, twid_sin = tables
    real_p, imag_p = product
    joined = jnp.concatenate([real_p, imag_p], axis=2)
    section_q = jnp.einsum("rkn,nm->rkm", joined, right_inv, preferred_element_type=jnp.float32)
    real_q = section_q[:, :, :radix]
    imag_q = section_q[:, :, radix:]
    real_r = (real_q * twid_cos - imag_q * twid_sin).astype(jnp.bfloat16)
    imag_r = (imag_q * twid_cos + real_q * twid_sin).astype(jnp.bfloat16)
    rows_both = jnp.concatenate([real_r, imag_r], axis=1)
    output = jnp.einsum("kn,rkm->rnm", left_table, rows_both, preferred_element_type=jnp.float32)
    count = real_p.shape[0]
    return (output * (1.0 / (freq_rows * radix))).reshape(count, freq_rows // 2 * radix)


def spectral_product(left, right, conj_left, conj_right):
    sign_left = -1.0 if conj_left else 1.0
    sign_right = -1.0 if conj_right else 1.0
    real_part = left[0] * right[0] - sign_left * sign_right * left[1] * right[1]
    imag_part = sign_left * left[1] * right[0] + sign_right * left[0] * right[1]
    return (real_part.astype(jnp.bfloat16), imag_part.astype(jnp.bfloat16))


def positional_features(positions, seq_len, bands):
    band_index = jnp.arange(1, bands + 1, dtype=jnp.int32)
    angles = (band_index[:, None] * positions[None, :] % seq_len).astype(jnp.float32) * (
        2.0 * math.pi / seq_len
    )
    ramp = positions.astype(jnp.float32)[None, :] / seq_len
    return jnp.concatenate([ramp, jnp.cos(angles), jnp.sin(angles)], axis=0)


def filter_network(positions, seq_len, pos_weight, pos_bias, mid_weight, mid_bias):
    bands = (pos_weight.shape[1] - 1) // 2
    features = positional_features(positions, seq_len, bands)
    pre_one = jnp.dot(pos_weight, features, precision=lax.Precision.HIGHEST) + pos_bias[:, None]
    act_one = jnp.sin(pre_one)
    pre_two = jnp.dot(mid_weight, act_one, precision=lax.Precision.HIGHEST) + mid_bias[:, None]
    act_two = jnp.sin(pre_two)
    return (features, pre_one, act_one, pre_two, act_two)


def modulation(rates, positions, seq_len):
    return jnp.exp(-rates[:, None] * positions.astype(jnp.float32)[None, :] / seq_len)


def contract_last(left, right):
    return lax.dot_general(left, right, (((1,), (1,)), ((), ())), precision=lax.Precision.HIGHEST)


def network_backward(act_grad, features, pre_one, act_one, pre_two, mid_weight):
    pre_two_grad = act_grad * jnp.cos(pre_two)
    mid_weight_part = contract_last(pre_two_grad, act_one)
    mid_bias_part = jnp.sum(pre_two_grad, axis=1)
    pre_one_grad = jnp.dot(mid_weight.T, pre_two_grad, precision=lax.Precision.HIGHEST) * jnp.cos(
        pre_one
    )
    pos_weight_part = contract_last(pre_one_grad, features)
    pos_bias_part = jnp.sum(pre_one_grad, axis=1)
    return (pos_weight_part, pos_bias_part, mid_weight_part, mid_bias_part)


def on_device_plain(
    value_branch,
    first_gate,
    second_gate,
    out_cotangent,
    pos_weight,
    pos_bias,
    mid_weight,
    mid_bias,
    out_weight,
    decay_rates,
):
    model_width, tok_dev = value_branch.shape
    devices = lax.axis_size("seq")
    seq_len = tok_dev * devices
    channels = model_width // devices
    my_rank = lax.axis_index("seq")
    freq_rows = 2 * seq_len // RADIX
    tables = make_tables(freq_rows, RADIX)
    all_positions = jnp.arange(seq_len, dtype=jnp.int32)
    own_rates = lax.dynamic_slice_in_dim(decay_rates, my_rank * 2 * channels, 2 * channels)
    window_own = modulation(own_rates, all_positions, seq_len)
    value_ch, first_ch = (
        lax.all_to_all(value_branch, "seq", split_axis=0, concat_axis=1, tiled=True),
        lax.all_to_all(first_gate, "seq", split_axis=0, concat_axis=1, tiled=True),
    )
    local_positions = my_rank * tok_dev + jnp.arange(tok_dev, dtype=jnp.int32)
    features, pre_one, act_one, pre_two, act_two = filter_network(
        local_positions, seq_len, pos_weight, pos_bias, mid_weight, mid_bias
    )
    window_local = modulation(decay_rates, local_positions, seq_len)
    local_filters = (
        jnp.dot(out_weight, act_two, precision=lax.Precision.HIGHEST) * window_local
    ).astype(jnp.bfloat16)
    filt_ch = lax.all_to_all(local_filters, "seq", split_axis=0, concat_axis=1, tiled=True)
    filt_real, filt_imag = forward_spectrum(filt_ch, tables, freq_rows, RADIX)
    filt_real = filt_real.reshape(channels, 2, freq_rows, RADIX)
    filt_imag = filt_imag.reshape(channels, 2, freq_rows, RADIX)
    spec_one = (filt_real[:, 0], filt_imag[:, 0])
    spec_two = (filt_real[:, 1], filt_imag[:, 1])
    spec_val = forward_spectrum(value_ch, tables, freq_rows, RADIX)
    conv_one = inverse_signal(
        spectral_product(spec_one, spec_val, False, False), tables, freq_rows, RADIX
    )
    gated = (first_ch.astype(jnp.float32) * conv_one).astype(jnp.bfloat16)
    spec_gated = forward_spectrum(gated, tables, freq_rows, RADIX)
    conv_two = inverse_signal(
        spectral_product(spec_two, spec_gated, False, False), tables, freq_rows, RADIX
    )
    second_ch, cot_ch = (
        lax.all_to_all(second_gate, "seq", split_axis=0, concat_axis=1, tiled=True),
        lax.all_to_all(out_cotangent, "seq", split_axis=0, concat_axis=1, tiled=True),
    )
    cot_wide = cot_ch.astype(jnp.float32)
    second_grad_ch = (cot_wide * conv_two).astype(jnp.bfloat16)
    second_out = lax.all_to_all(second_grad_ch, "seq", split_axis=1, concat_axis=0, tiled=True)
    grad_two = (cot_wide * second_ch.astype(jnp.float32)).astype(jnp.bfloat16)
    spec_gtwo = forward_spectrum(grad_two, tables, freq_rows, RADIX)
    gated_grad = inverse_signal(
        spectral_product(spec_two, spec_gtwo, True, False), tables, freq_rows, RADIX
    )
    filt_grad_two = inverse_signal(
        spectral_product(spec_gtwo, spec_gated, False, True), tables, freq_rows, RADIX
    )
    first_grad_ch = (gated_grad * conv_one).astype(jnp.bfloat16)
    grad_one = (gated_grad * first_ch.astype(jnp.float32)).astype(jnp.bfloat16)
    spec_gone = forward_spectrum(grad_one, tables, freq_rows, RADIX)
    value_grad_ch = inverse_signal(
        spectral_product(spec_one, spec_gone, True, False), tables, freq_rows, RADIX
    ).astype(jnp.bfloat16)
    filt_grad_one = inverse_signal(
        spectral_product(spec_gone, spec_val, False, True), tables, freq_rows, RADIX
    )
    value_out, first_out = (
        lax.all_to_all(value_grad_ch, "seq", split_axis=1, concat_axis=0, tiled=True),
        lax.all_to_all(first_grad_ch, "seq", split_axis=1, concat_axis=0, tiled=True),
    )
    filt_grads = jnp.stack([filt_grad_one, filt_grad_two], axis=1).reshape(2 * channels, seq_len)
    filter_grad_ch = filt_grads * window_own / seq_len
    filter_grad_seq = lax.all_to_all(
        filter_grad_ch.astype(jnp.bfloat16), "seq", split_axis=1, concat_axis=0, tiled=True
    ).astype(filter_grad_ch.dtype)
    out_weight_grad = lax.psum_scatter(
        contract_last(filter_grad_seq, act_two), "seq", scatter_dimension=0, tiled=True
    )
    act_grad = jnp.dot(out_weight.T, filter_grad_seq, precision=lax.Precision.HIGHEST)
    partials = network_backward(act_grad, features, pre_one, act_one, pre_two, mid_weight)
    pos_weight_grad, pos_bias_grad, mid_weight_grad, mid_bias_grad = lax.psum(
        (partials[0], partials[1], partials[2], partials[3]), "seq"
    )
    return (
        value_out,
        first_out,
        second_out,
        pos_weight_grad,
        pos_bias_grad,
        mid_weight_grad,
        mid_bias_grad,
        out_weight_grad,
    )


def numpy_tables(freq_rows, radix, seq_len, bands, group):
    half = freq_rows // 2
    length_all = freq_rows * radix
    freq_index = np.arange(freq_rows)
    inner = np.arange(radix)
    angle_one = (freq_index[:, None] * np.arange(half)[None, :] % freq_rows) * (2.0 * np.pi / freq_rows)
    angle_two = (inner[:, None] * inner[None, :] % radix) * (2.0 * np.pi / radix)
    angle_twid = (freq_index[:, None] * inner[None, :] % length_all) * (2.0 * np.pi / length_all)
    left = np.concatenate([np.cos(angle_one), -np.sin(angle_one)], axis=0)
    left_fwd = np.kron(left, np.eye(group))
    left_inv = left_fwd.T / length_all
    cos_two, sin_two = np.cos(angle_two), np.sin(angle_two)
    right_fwd = np.block([[cos_two, -sin_two], [sin_two, cos_two]])
    right_inv = np.block([[cos_two, sin_two], [-sin_two, cos_two]])
    twid_cos = np.repeat(np.cos(angle_twid), group, axis=0)
    twid_sin = np.repeat(np.sin(angle_twid), group, axis=0)
    positions = np.arange(seq_len)
    band = np.arange(1, bands + 1)
    angles = (band[:, None] * positions[None, :] % seq_len) * (2.0 * np.pi / seq_len)
    features = np.zeros((64, seq_len))
    features[0] = positions / seq_len
    features[1 : bands + 1] = np.cos(angles)
    features[bands + 1 : 2 * bands + 1] = np.sin(angles)
    features[2 * bands + 1] = 1.0
    low = [table.astype(ml_dtypes.bfloat16) for table in (left_fwd, left_inv, right_fwd, right_inv)]
    wide = [table.astype(np.float32) for table in (twid_cos, twid_sin, features)]
    return low + wide


def sin_cos(x):
    turns = jnp.floor(x * (1.0 / math.pi) + 0.5)
    rest = x - turns * 3.140625
    rest = rest - turns * 9.67502593994140625e-4
    rest = rest - turns * 1.509957990978376432e-7
    sign = 1.0 - 2.0 * (turns - 2.0 * jnp.floor(turns * 0.5))
    square = rest * rest
    odd = 1.0 / 6227020800.0
    for term in (-1.0 / 39916800.0, 1.0 / 362880.0, -1.0 / 5040.0, 1.0 / 120.0, -1.0 / 6.0, 1.0):
        odd = odd * square + term
    even = 1.0 / 479001600.0
    for term in (-1.0 / 3628800.0, 1.0 / 40320.0, -1.0 / 720.0, 1.0 / 24.0, -0.5, 1.0):
        even = even * square + term
    return sign * rest * odd, sign * even


def wide_dot(left, right):
    return jnp.dot(left, right, precision=HIGHEST, preferred_element_type=jnp.float32)


def short_dot(left, right):
    return jnp.dot(left, right, preferred_element_type=jnp.float32)


def contract_dims(left, right, left_dim, right_dim):
    return lax.dot_general(
        left,
        right,
        (((left_dim,), (right_dim,)), ((), ())),
        precision=HIGHEST,
        preferred_element_type=jnp.float32,
    )


def as_column(row, count):
    width = row.shape[1]
    diagonal = lax.broadcasted_iota(jnp.int32, (count, width), 0) == lax.broadcasted_iota(
        jnp.int32, (count, width), 1
    )
    return jnp.sum(jnp.where(diagonal, row, 0.0), axis=1, keepdims=True)


def operator_kernel(
    devices,
    channels,
    features_used,
    value_ref,
    first_ref,
    second_ref,
    cot_ref,
    pos_weight_ref,
    pos_bias_ref,
    mid_weight_ref,
    mid_bias_ref,
    out_weight_ref,
    rates_ref,
    left_fwd_ref,
    left_inv_ref,
    right_fwd_ref,
    right_inv_ref,
    twid_cos_ref,
    twid_sin_ref,
    features_ref,
    value_out,
    first_out,
    second_out,
    out_weight_out,
    small_out,
    recv,
    outs,
    small_part,
    small_recv,
    small_sum,
    in_send,
    in_recv,
    out_send,
    out_recv,
    part_send,
    part_recv,
    sum_send,
    sum_recv,
):
    n = devices
    me = lax.axis_index("seq")
    width = RADIX
    seq_len = n * width
    groups = channels // GROUP
    rows_half = 2 * n * GROUP
    half_rows = n * GROUP
    bf16 = jnp.bfloat16
    f32 = jnp.float32

    barrier = pltpu.get_barrier_semaphore()

    def greet(step, carry):
        pl.semaphore_signal(
            barrier, inc=1, device_id={"seq": lax.rem(me + step, n)}, device_id_type=MESH
        )
        return carry

    lax.fori_loop(1, n, greet, 0)
    pl.semaphore_wait(barrier, n - 1)

    inputs = (value_ref, first_ref, cot_ref, second_ref)
    outputs = (second_out, first_out, value_out)

    def in_copy(at, peer, slot):
        return pltpu.make_async_remote_copy(
            src_ref=inputs[at].at[pl.ds(pl.multiple_of(peer * channels, channels), channels), :],
            dst_ref=recv.at[at, slot],
            send_sem=in_send.at[at, peer],
            recv_sem=in_recv.at[at, slot],
            device_id={"seq": peer},
            device_id_type=MESH,
        )

    def out_copy(at, peer, slot):
        return pltpu.make_async_remote_copy(
            src_ref=outs.at[at, peer],
            dst_ref=outputs[at].at[pl.ds(pl.multiple_of(slot * channels, channels), channels), :],
            send_sem=out_send.at[at, peer],
            recv_sem=out_recv.at[at, slot],
            device_id={"seq": peer},
            device_id_type=MESH,
        )

    def part_copy(peer, slot):
        return pltpu.make_async_remote_copy(
            src_ref=small_part.at[peer],
            dst_ref=small_recv.at[slot],
            send_sem=part_send.at[peer],
            recv_sem=part_recv.at[slot],
            device_id={"seq": peer},
            device_id_type=MESH,
        )

    def sum_copy(peer, slot):
        return pltpu.make_async_remote_copy(
            src_ref=small_sum,
            dst_ref=small_out.at[slot],
            send_sem=sum_send.at[peer],
            recv_sem=sum_recv.at[slot],
            device_id={"seq": peer},
            device_id_type=MESH,
        )

    def for_peers(action):
        def body(step, carry):
            action(lax.rem(me + step, n))
            return carry

        lax.fori_loop(1, n, body, 0)

    for at in range(4):
        for_peers(lambda peer, at=at: in_copy(at, peer, me).start())
    own_rows = pl.ds(pl.multiple_of(me * channels, channels), channels)
    for at in range(4):
        recv[at, me] = inputs[at][own_rows, :]

    features = features_ref[...]
    pre_one = wide_dot(pos_weight_ref[...], features_ref[0:features_used, :]) + as_column(
        pos_bias_ref[...], 64
    )
    act_one, slope_one = sin_cos(pre_one)
    pre_two = wide_dot(mid_weight_ref[...], act_one) + as_column(mid_bias_ref[...], 64)
    act_two, slope_two = sin_cos(pre_two)

    first_row = me * (2 * channels)
    own_weight = jnp.concatenate(
        [out_weight_ref[pl.ds(first_row + o, channels, stride=2), :] for o in range(2)], axis=0
    )
    filter_rows = rates_ref.shape[1]
    lane = lax.broadcasted_iota(jnp.int32, (2 * channels, filter_rows), 1)
    row = lax.broadcasted_iota(jnp.int32, (2 * channels, filter_rows), 0)
    wanted = jnp.where(row < channels, 2 * row, 2 * (row - channels) + 1) + first_row
    own_rates = jnp.sum(jnp.where(lane == wanted, rates_ref[...], 0.0), axis=1, keepdims=True)
    ramp = lax.broadcasted_iota(jnp.int32, (1, seq_len), 1).astype(f32) * (1.0 / seq_len)
    window = jnp.exp(-own_rates * ramp)
    filters = (wide_dot(own_weight, act_two) * window).astype(bf16)

    def to_sections(rows):
        return jnp.concatenate(
            [
                jnp.concatenate(
                    [
                        rows[GROUP * g : GROUP * (g + 1), width * at : width * (at + 1)]
                        for at in range(n)
                    ],
                    axis=0,
                )
                for g in range(groups)
            ],
            axis=1,
        )

    def from_sections(data):
        return jnp.concatenate(
            [
                jnp.concatenate(
                    [
                        data[GROUP * at : GROUP * (at + 1), width * g : width * (g + 1)]
                        for at in range(n)
                    ],
                    axis=1,
                )
                for g in range(groups)
            ],
            axis=0,
        )

    def forward(data):
        stage = short_dot(left_fwd_ref[...], data)
        cos, sin = twid_cos_ref[...], twid_sin_ref[...]
        result = []
        for g in range(groups):
            real = stage[:rows_half, width * g : width * (g + 1)]
            imag = stage[rows_half:, width * g : width * (g + 1)]
            real_b = (real * cos + imag * sin).astype(bf16)
            imag_b = (imag * cos - real * sin).astype(bf16)
            spectrum = short_dot(jnp.concatenate([real_b, imag_b], axis=1), right_fwd_ref[...])
            result.append((spectrum[:, :width], spectrum[:, width:]))
        return result

    def inverse(left, right, conj_left, conj_right):
        cos, sin = twid_cos_ref[...], twid_sin_ref[...]
        sections = []
        for g in range(groups):
            real_p, imag_p = spectral_product(left[g], right[g], conj_left, conj_right)
            stage = short_dot(jnp.concatenate([real_p, imag_p], axis=1), right_inv_ref[...])
            real, imag = stage[:, :width], stage[:, width:]
            real_r = (real * cos - imag * sin).astype(bf16)
            imag_r = (imag * cos + real * sin).astype(bf16)
            sections.append(jnp.concatenate([real_r, imag_r], axis=0))
        return short_dot(left_inv_ref[...], jnp.concatenate(sections, axis=1))

    def arrived(at):
        for_peers(lambda peer: in_copy(at, peer, peer).wait_recv())
        return jnp.concatenate(
            [
                recv[at, :, GROUP * g : GROUP * (g + 1), :].reshape(half_rows, width)
                for g in range(groups)
            ],
            axis=1,
        )

    def send_out(at, data):
        for g in range(groups):
            outs[at, :, GROUP * g : GROUP * (g + 1), :] = data[
                :, width * g : width * (g + 1)
            ].reshape(n, GROUP, width)
        for_peers(lambda peer: out_copy(at, peer, me).start())
        outputs[at][own_rows, :] = outs[at, me]

    spec_one = forward(to_sections(filters[:channels]))
    spec_two = forward(to_sections(filters[channels:]))
    spec_val = forward(arrived(0))
    conv_one = inverse(spec_one, spec_val, False, False)
    first = arrived(1).astype(f32)
    spec_gated = forward((first * conv_one).astype(bf16))
    conv_two = inverse(spec_two, spec_gated, False, False)
    cot = arrived(2).astype(f32)
    send_out(0, (cot * conv_two).astype(bf16))
    second = arrived(3).astype(f32)
    spec_gtwo = forward((cot * second).astype(bf16))
    gated_grad = inverse(spec_two, spec_gtwo, True, False)
    send_out(1, (gated_grad * conv_one).astype(bf16))
    spec_gone = forward((gated_grad * first).astype(bf16))
    send_out(2, inverse(spec_one, spec_gone, True, False).astype(bf16))
    filt_one = from_sections(inverse(spec_gone, spec_val, False, True))
    filt_two = from_sections(inverse(spec_gtwo, spec_gated, False, True))
    filter_grad = jnp.concatenate([filt_one, filt_two], axis=0) * window * (1.0 / seq_len)

    pre_two_grad = contract_dims(own_weight, filter_grad, 0, 0) * slope_two
    pre_one_grad = contract_dims(mid_weight_ref[...], pre_two_grad, 0, 0) * slope_one
    ones_row = jnp.where(
        lax.broadcasted_iota(jnp.int32, (64, seq_len), 0) == features_used + 1, 1.0, 0.0
    )
    small = contract_dims(pre_two_grad, jnp.concatenate([act_one, ones_row], axis=0), 1, 1)
    small = small + contract_dims(
        pre_one_grad, jnp.concatenate([jnp.zeros_like(features), features], axis=0), 1, 1
    )
    share = small.shape[0] // n
    for at in range(n):
        small_part[at] = small[share * at : share * (at + 1), :]
    for_peers(lambda peer: part_copy(peer, me).start())
    small_recv[me] = small_part[me]

    weight_grad = contract_dims(filter_grad, act_two, 1, 1)
    for o in range(2):
        out_weight_out[pl.ds(o, channels, stride=2), :] = weight_grad[
            channels * o : channels * (o + 1)
        ]

    for_peers(lambda peer: part_copy(peer, peer).wait_recv())
    total = small_recv[0]
    for at in range(1, n):
        total = total + small_recv[at]
    small_sum[...] = total
    small_out[me] = total
    for_peers(lambda peer: sum_copy(peer, me).start())

    for at in range(4):
        for_peers(lambda peer, at=at: in_copy(at, peer, me).wait_send())
    for at in range(3):
        for_peers(lambda peer, at=at: out_copy(at, peer, me).wait_send())
        for_peers(lambda peer, at=at: out_copy(at, peer, peer).wait_recv())
    for_peers(lambda peer: part_copy(peer, me).wait_send())
    for_peers(lambda peer: sum_copy(peer, me).wait_send())
    for_peers(lambda peer: sum_copy(peer, peer).wait_recv())


def on_device(
    value_branch,
    first_gate,
    second_gate,
    out_cotangent,
    pos_weight,
    pos_bias,
    mid_weight,
    mid_bias,
    out_weight,
    decay_rates,
):
    model_width, tok_dev = value_branch.shape
    devices = lax.axis_size("seq")
    channels = model_width // devices
    hidden, features_used = pos_weight.shape
    fits = (
        tok_dev == RADIX
        and devices == 16
        and channels == 2 * GROUP
        and hidden == 64
        and features_used <= 62
        and out_weight.shape == (2 * model_width, 64)
    )
    if not fits:
        return on_device_plain(
            value_branch,
            first_gate,
            second_gate,
            out_cotangent,
            pos_weight,
            pos_bias,
            mid_weight,
            mid_bias,
            out_weight,
            decay_rates,
        )
    seq_len = tok_dev * devices
    freq_rows = 2 * devices
    tables = numpy_tables(freq_rows, RADIX, seq_len, (features_used - 1) // 2, GROUP)
    share = hidden // devices
    dma = pltpu.SemaphoreType.DMA
    vmem = pl.BlockSpec(memory_space=pltpu.VMEM)
    value_out, first_out, second_out, weight_out, small = pl.pallas_call(
        functools.partial(operator_kernel, devices, channels, features_used),
        out_shape=[jax.ShapeDtypeStruct((model_width, tok_dev), jnp.bfloat16)] * 3
        + [
            jax.ShapeDtypeStruct((2 * channels, hidden), jnp.float32),
            jax.ShapeDtypeStruct((devices, share, 2 * hidden), jnp.float32),
        ],
        in_specs=[vmem] * 17,
        out_specs=[vmem] * 5,
        scratch_shapes=[
            pltpu.VMEM((4, devices, channels, RADIX), jnp.bfloat16),
            pltpu.VMEM((3, devices, channels, RADIX), jnp.bfloat16),
            pltpu.VMEM((devices, share, 2 * hidden), jnp.float32),
            pltpu.VMEM((devices, share, 2 * hidden), jnp.float32),
            pltpu.VMEM((share, 2 * hidden), jnp.float32),
            dma((4, devices)),
            dma((4, devices)),
            dma((3, devices)),
            dma((3, devices)),
            dma((devices,)),
            dma((devices,)),
            dma((devices,)),
            dma((devices,)),
        ],
        compiler_params=pltpu.CompilerParams(
            collective_id=0, has_side_effects=True, vmem_limit_bytes=50 * 1024 * 1024
        ),
    )(
        value_branch,
        first_gate,
        second_gate,
        out_cotangent,
        pos_weight,
        pos_bias.reshape(1, hidden),
        mid_weight,
        mid_bias.reshape(1, hidden),
        out_weight,
        decay_rates.reshape(1, 2 * model_width),
        *[jnp.asarray(table) for table in tables],
    )
    small = small.reshape(hidden, 2 * hidden)
    at = hidden + features_used
    return (
        value_out,
        first_out,
        second_out,
        small[:, hidden:at],
        small[:, at],
        small[:, :hidden],
        small[:, at + 1],
        weight_out,
    )


def solution(mesh):
    in_specs = (
        P(None, ("dp", "seq")),
        P(None, ("dp", "seq")),
        P(None, ("dp", "seq")),
        P(None, ("dp", "seq")),
        P(),
        P(),
        P(),
        P(),
        P(),
        P(),
    )
    out_specs = (
        P(None, ("dp", "seq")),
        P(None, ("dp", "seq")),
        P(None, ("dp", "seq")),
        P("dp", None),
        P("dp"),
        P("dp", None),
        P("dp"),
        P("seq", "dp"),
    )
    return jax.shard_map(
        on_device, mesh=mesh, in_specs=in_specs, out_specs=out_specs, check_vma=False
    )
```

```python
import functools
import math

import jax
import jax.numpy as jnp
import ml_dtypes
import numpy as np
from jax import lax
from jax.experimental import pallas as pl
from jax.experimental.pallas import tpu as pltpu
from jax.sharding import PartitionSpec as P

RADIX = 128
GROUP = 16
MESH = pl.DeviceIdType.MESH


def make_tables(freq_rows, radix):
    length_all = freq_rows * radix
    freq_index = jnp.arange(freq_rows, dtype=jnp.int32)
    half_index = jnp.arange(freq_rows // 2, dtype=jnp.int32)
    inner_index = jnp.arange(radix, dtype=jnp.int32)
    angle_one = (freq_index[:, None] * half_index[None, :] % freq_rows).astype(jnp.float32) * (
        2.0 * math.pi / freq_rows
    )
    angle_two = (inner_index[:, None] * inner_index[None, :] % radix).astype(jnp.float32) * (
        2.0 * math.pi / radix
    )
    angle_twid = (freq_index[:, None] * inner_index[None, :] % length_all).astype(jnp.float32) * (
        2.0 * math.pi / length_all
    )
    cos_one = jnp.cos(angle_one).astype(jnp.bfloat16)
    sin_one = jnp.sin(angle_one).astype(jnp.bfloat16)
    cos_two = jnp.cos(angle_two).astype(jnp.bfloat16)
    sin_two = jnp.sin(angle_two).astype(jnp.bfloat16)
    left_table = jnp.concatenate([cos_one, -sin_one], axis=0)
    right_fwd = jnp.concatenate(
        [jnp.concatenate([cos_two, -sin_two], axis=1), jnp.concatenate([sin_two, cos_two], axis=1)],
        axis=0,
    )
    right_inv = jnp.concatenate(
        [jnp.concatenate([cos_two, sin_two], axis=1), jnp.concatenate([-sin_two, cos_two], axis=1)],
        axis=0,
    )
    return (left_table, right_fwd, right_inv, jnp.cos(angle_twid), jnp.sin(angle_twid))


def forward_spectrum(signal, tables, freq_rows, radix):
    left_table, right_fwd, right_inv, twid_cos, twid_sin = tables
    count = signal.shape[0]
    shaped = signal.reshape(count, freq_rows // 2, radix)
    stacked = jnp.einsum("kn,rnm->rkm", left_table, shaped, preferred_element_type=jnp.float32)
    real_a = stacked[:, :freq_rows]
    imag_a = stacked[:, freq_rows:]
    real_b = (real_a * twid_cos + imag_a * twid_sin).astype(jnp.bfloat16)
    imag_b = (imag_a * twid_cos - real_a * twid_sin).astype(jnp.bfloat16)
    joined = jnp.concatenate([real_b, imag_b], axis=2)
    spectrum = jnp.einsum("rkn,nm->rkm", joined, right_fwd, preferred_element_type=jnp.float32)
    return (spectrum[:, :, :radix], spectrum[:, :, radix:])


def inverse_signal(product, tables, freq_rows, radix):
    left_table, right_fwd, right_inv, twid_cos, twid_sin = tables
    real_p, imag_p = product
    joined = jnp.concatenate([real_p, imag_p], axis=2)
    section_q = jnp.einsum("rkn,nm->rkm", joined, right_inv, preferred_element_type=jnp.float32)
    real_q = section_q[:, :, :radix]
    imag_q = section_q[:, :, radix:]
    real_r = (real_q * twid_cos - imag_q * twid_sin).astype(jnp.bfloat16)
    imag_r = (imag_q * twid_cos + real_q * twid_sin).astype(jnp.bfloat16)
    rows_both = jnp.concatenate([real_r, imag_r], axis=1)
    output = jnp.einsum("kn,rkm->rnm", left_table, rows_both, preferred_element_type=jnp.float32)
    count = real_p.shape[0]
    return (output * (1.0 / (freq_rows * radix))).reshape(count, freq_rows // 2 * radix)


def spectral_product(left, right, conj_left, conj_right):
    sign_left = -1.0 if conj_left else 1.0
    sign_right = -1.0 if conj_right else 1.0
    real_part = left[0] * right[0] - sign_left * sign_right * left[1] * right[1]
    imag_part = sign_left * left[1] * right[0] + sign_right * left[0] * right[1]
    return (real_part.astype(jnp.bfloat16), imag_part.astype(jnp.bfloat16))


def positional_features(positions, seq_len, bands):
    band_index = jnp.arange(1, bands + 1, dtype=jnp.int32)
    angles = (band_index[:, None] * positions[None, :] % seq_len).astype(jnp.float32) * (
        2.0 * math.pi / seq_len
    )
    ramp = positions.astype(jnp.float32)[None, :] / seq_len
    return jnp.concatenate([ramp, jnp.cos(angles), jnp.sin(angles)], axis=0)


def filter_network(positions, seq_len, pos_weight, pos_bias, mid_weight, mid_bias):
    bands = (pos_weight.shape[1] - 1) // 2
    features = positional_features(positions, seq_len, bands)
    pre_one = jnp.dot(pos_weight, features, precision=lax.Precision.HIGHEST) + pos_bias[:, None]
    act_one = jnp.sin(pre_one)
    pre_two = jnp.dot(mid_weight, act_one, precision=lax.Precision.HIGHEST) + mid_bias[:, None]
    act_two = jnp.sin(pre_two)
    return (features, pre_one, act_one, pre_two, act_two)


def modulation(rates, positions, seq_len):
    return jnp.exp(-rates[:, None] * positions.astype(jnp.float32)[None, :] / seq_len)


def contract_last(left, right):
    return lax.dot_general(left, right, (((1,), (1,)), ((), ())), precision=lax.Precision.HIGHEST)


def network_backward(act_grad, features, pre_one, act_one, pre_two, mid_weight):
    pre_two_grad = act_grad * jnp.cos(pre_two)
    mid_weight_part = contract_last(pre_two_grad, act_one)
    mid_bias_part = jnp.sum(pre_two_grad, axis=1)
    pre_one_grad = jnp.dot(mid_weight.T, pre_two_grad, precision=lax.Precision.HIGHEST) * jnp.cos(
        pre_one
    )
    pos_weight_part = contract_last(pre_one_grad, features)
    pos_bias_part = jnp.sum(pre_one_grad, axis=1)
    return (pos_weight_part, pos_bias_part, mid_weight_part, mid_bias_part)


def on_device_plain(
    value_branch,
    first_gate,
    second_gate,
    out_cotangent,
    pos_weight,
    pos_bias,
    mid_weight,
    mid_bias,
    out_weight,
    decay_rates,
):
    model_width, tok_dev = value_branch.shape
    devices = lax.axis_size("seq")
    seq_len = tok_dev * devices
    channels = model_width // devices
    my_rank = lax.axis_index("seq")
    freq_rows = 2 * seq_len // RADIX
    tables = make_tables(freq_rows, RADIX)
    all_positions = jnp.arange(seq_len, dtype=jnp.int32)
    own_rates = lax.dynamic_slice_in_dim(decay_rates, my_rank * 2 * channels, 2 * channels)
    window_own = modulation(own_rates, all_positions, seq_len)
    value_ch, first_ch = (
        lax.all_to_all(value_branch, "seq", split_axis=0, concat_axis=1, tiled=True),
        lax.all_to_all(first_gate, "seq", split_axis=0, concat_axis=1, tiled=True),
    )
    local_positions = my_rank * tok_dev + jnp.arange(tok_dev, dtype=jnp.int32)
    features, pre_one, act_one, pre_two, act_two = filter_network(
        local_positions, seq_len, pos_weight, pos_bias, mid_weight, mid_bias
    )
    window_local = modulation(decay_rates, local_positions, seq_len)
    local_filters = (
        jnp.dot(out_weight, act_two, precision=lax.Precision.HIGHEST) * window_local
    ).astype(jnp.bfloat16)
    filt_ch = lax.all_to_all(local_filters, "seq", split_axis=0, concat_axis=1, tiled=True)
    filt_real, filt_imag = forward_spectrum(filt_ch, tables, freq_rows, RADIX)
    filt_real = filt_real.reshape(channels, 2, freq_rows, RADIX)
    filt_imag = filt_imag.reshape(channels, 2, freq_rows, RADIX)
    spec_one = (filt_real[:, 0], filt_imag[:, 0])
    spec_two = (filt_real[:, 1], filt_imag[:, 1])
    spec_val = forward_spectrum(value_ch, tables, freq_rows, RADIX)
    conv_one = inverse_signal(
        spectral_product(spec_one, spec_val, False, False), tables, freq_rows, RADIX
    )
    gated = (first_ch.astype(jnp.float32) * conv_one).astype(jnp.bfloat16)
    spec_gated = forward_spectrum(gated, tables, freq_rows, RADIX)
    conv_two = inverse_signal(
        spectral_product(spec_two, spec_gated, False, False), tables, freq_rows, RADIX
    )
    second_ch, cot_ch = (
        lax.all_to_all(second_gate, "seq", split_axis=0, concat_axis=1, tiled=True),
        lax.all_to_all(out_cotangent, "seq", split_axis=0, concat_axis=1, tiled=True),
    )
    cot_wide = cot_ch.astype(jnp.float32)
    second_grad_ch = (cot_wide * conv_two).astype(jnp.bfloat16)
    second_out = lax.all_to_all(second_grad_ch, "seq", split_axis=1, concat_axis=0, tiled=True)
    grad_two = (cot_wide * second_ch.astype(jnp.float32)).astype(jnp.bfloat16)
    spec_gtwo = forward_spectrum(grad_two, tables, freq_rows, RADIX)
    gated_grad = inverse_signal(
        spectral_product(spec_two, spec_gtwo, True, False), tables, freq_rows, RADIX
    )
    filt_grad_two = inverse_signal(
        spectral_product(spec_gtwo, spec_gated, False, True), tables, freq_rows, RADIX
    )
    first_grad_ch = (gated_grad * conv_one).astype(jnp.bfloat16)
    grad_one = (gated_grad * first_ch.astype(jnp.float32)).astype(jnp.bfloat16)
    spec_gone = forward_spectrum(grad_one, tables, freq_rows, RADIX)
    value_grad_ch = inverse_signal(
        spectral_product(spec_one, spec_gone, True, False), tables, freq_rows, RADIX
    ).astype(jnp.bfloat16)
    filt_grad_one = inverse_signal(
        spectral_product(spec_gone, spec_val, False, True), tables, freq_rows, RADIX
    )
    value_out, first_out = (
        lax.all_to_all(value_grad_ch, "seq", split_axis=1, concat_axis=0, tiled=True),
        lax.all_to_all(first_grad_ch, "seq", split_axis=1, concat_axis=0, tiled=True),
    )
    filt_grads = jnp.stack([filt_grad_one, filt_grad_two], axis=1).reshape(2 * channels, seq_len)
    filter_grad_ch = filt_grads * window_own / seq_len
    filter_grad_seq = lax.all_to_all(
        filter_grad_ch.astype(jnp.bfloat16), "seq", split_axis=1, concat_axis=0, tiled=True
    ).astype(filter_grad_ch.dtype)
    out_weight_grad = lax.psum_scatter(
        contract_last(filter_grad_seq, act_two), "seq", scatter_dimension=0, tiled=True
    )
    act_grad = jnp.dot(out_weight.T, filter_grad_seq, precision=lax.Precision.HIGHEST)
    partials = network_backward(act_grad, features, pre_one, act_one, pre_two, mid_weight)
    pos_weight_grad, pos_bias_grad, mid_weight_grad, mid_bias_grad = lax.psum(
        (partials[0], partials[1], partials[2], partials[3]), "seq"
    )
    return (
        value_out,
        first_out,
        second_out,
        pos_weight_grad,
        pos_bias_grad,
        mid_weight_grad,
        mid_bias_grad,
        out_weight_grad,
    )


def numpy_tables(freq_rows, radix, seq_len, bands, group):
    half = freq_rows // 2
    length_all = freq_rows * radix
    freq_index = np.arange(freq_rows)
    inner = np.arange(radix)
    angle_one = (freq_index[:, None] * np.arange(half)[None, :] % freq_rows) * (2.0 * np.pi / freq_rows)
    angle_two = (inner[:, None] * inner[None, :] % radix) * (2.0 * np.pi / radix)
    angle_twid = (freq_index[:, None] * inner[None, :] % length_all) * (2.0 * np.pi / length_all)
    left = np.concatenate([np.cos(angle_one), -np.sin(angle_one)], axis=0)
    left_fwd = np.kron(left, np.eye(group))
    left_inv = left_fwd.T / length_all
    cos_two, sin_two = np.cos(angle_two), np.sin(angle_two)
    right_fwd = np.block([[cos_two, -sin_two], [sin_two, cos_two]])
    right_inv = np.block([[cos_two, sin_two], [-sin_two, cos_two]])
    twid_cos = np.repeat(np.cos(angle_twid), group, axis=0)
    twid_sin = np.repeat(np.sin(angle_twid), group, axis=0)
    positions = np.arange(seq_len)
    band = np.arange(1, bands + 1)
    angles = (band[:, None] * positions[None, :] % seq_len) * (2.0 * np.pi / seq_len)
    features = np.zeros((64, seq_len), np.float32)
    features[0] = positions / seq_len
    features[1 : bands + 1] = np.cos(angles)
    features[bands + 1 : 2 * bands + 1] = np.sin(angles)
    features[2 * bands + 1 : 2 * bands + 3] = 1.0
    upper = features.astype(ml_dtypes.bfloat16)
    lower = (features - upper.astype(np.float32)).astype(ml_dtypes.bfloat16)
    features = np.concatenate([upper, lower], axis=0)
    low = [table.astype(ml_dtypes.bfloat16) for table in (left_fwd, left_inv, right_fwd, right_inv)]
    wide = [table.astype(np.float32) for table in (twid_cos, twid_sin)]
    return low + wide + [features]


def sin_cos(x):
    turns = jnp.floor(x * (1.0 / math.pi) + 0.5)
    rest = x - turns * 3.140625
    rest = rest - turns * 9.67502593994140625e-4
    rest = rest - turns * 1.509957990978376432e-7
    sign = 1.0 - 2.0 * (turns - 2.0 * jnp.floor(turns * 0.5))
    square = rest * rest
    odd = 1.0 / 6227020800.0
    for term in (-1.0 / 39916800.0, 1.0 / 362880.0, -1.0 / 5040.0, 1.0 / 120.0, -1.0 / 6.0, 1.0):
        odd = odd * square + term
    even = 1.0 / 479001600.0
    for term in (-1.0 / 3628800.0, 1.0 / 40320.0, -1.0 / 720.0, 1.0 / 24.0, -0.5, 1.0):
        even = even * square + term
    return sign * rest * odd, sign * even


def short_dot(left, right):
    return jnp.dot(left, right, preferred_element_type=jnp.float32)


def contract_dims(left, right, left_dim, right_dim):
    return lax.dot_general(
        left, right, (((left_dim,), (right_dim,)), ((), ())), preferred_element_type=jnp.float32
    )


def halves(x):
    upper = x.astype(jnp.bfloat16)
    return upper, (x - upper.astype(jnp.float32)).astype(jnp.bfloat16)


def split_dot(left, right):
    return contract_dims(
        jnp.concatenate([left[0], left[1], left[0]], axis=0),
        jnp.concatenate([right[0], right[0], right[1]], axis=0),
        0,
        0,
    )


def as_column(row, count):
    width = row.shape[1]
    diagonal = lax.broadcasted_iota(jnp.int32, (count, width), 0) == lax.broadcasted_iota(
        jnp.int32, (count, width), 1
    )
    return jnp.sum(jnp.where(diagonal, row, 0.0), axis=1, keepdims=True)


def operator_kernel(
    devices,
    channels,
    features_used,
    value_ref,
    first_ref,
    second_ref,
    cot_ref,
    pos_weight_hbm,
    pos_bias_hbm,
    mid_weight_hbm,
    mid_bias_hbm,
    out_weight_hbm,
    rates_hbm,
    left_fwd_hbm,
    left_inv_hbm,
    right_fwd_hbm,
    right_inv_hbm,
    twid_cos_hbm,
    twid_sin_hbm,
    features_hbm,
    value_out,
    first_out,
    second_out,
    out_weight_out,
    small_out,
    recv,
    outs,
    small_part,
    small_recv,
    small_sum,
    in_send,
    in_recv,
    out_send,
    out_recv,
    part_send,
    part_recv,
    sum_send,
    sum_recv,
    pos_weight_ref,
    pos_bias_ref,
    mid_weight_ref,
    mid_bias_ref,
    out_weight_ref,
    rates_ref,
    left_fwd_ref,
    left_inv_ref,
    right_fwd_ref,
    right_inv_ref,
    twid_cos_ref,
    twid_sin_ref,
    features_ref,
    pos_table,
    load_sem,
    own_sem,
):
    n = devices
    me = lax.axis_index("seq")
    width = RADIX
    seq_len = n * width
    groups = channels // GROUP
    rows_half = 2 * n * GROUP
    half_rows = n * GROUP
    bf16 = jnp.bfloat16
    f32 = jnp.float32

    barrier = pltpu.get_barrier_semaphore()

    def greet(step, carry):
        pl.semaphore_signal(
            barrier, inc=1, device_id={"seq": lax.rem(me + step, n)}, device_id_type=MESH
        )
        return carry

    lax.fori_loop(1, n, greet, 0)

    inputs = (value_ref, first_ref, cot_ref, second_ref)
    own_rows = pl.ds(pl.multiple_of(me * channels, channels), channels)
    pair = lax.rem(me, 2)
    column = me // 2
    loads = [
        pltpu.make_async_copy(source, target, load_sem.at[at])
        for at, (source, target) in enumerate(
            (
                (pos_weight_hbm, pos_weight_ref),
                (pos_bias_hbm, pos_bias_ref),
                (features_hbm, features_ref),
                (mid_weight_hbm, mid_weight_ref),
                (mid_bias_hbm, mid_bias_ref),
                (out_weight_hbm.at[:, pl.ds(pl.multiple_of(column * 128, 128), 128)], out_weight_ref),
                (rates_hbm, rates_ref),
                (left_fwd_hbm, left_fwd_ref),
                (right_fwd_hbm, right_fwd_ref),
                (twid_cos_hbm, twid_cos_ref),
                (twid_sin_hbm, twid_sin_ref),
                (right_inv_hbm, right_inv_ref),
                (left_inv_hbm, left_inv_ref),
            )
        )
    ]
    for load in loads:
        load.start()
    own_loads = [
        pltpu.make_async_copy(inputs[at].at[own_rows, :], recv.at[at, me], own_sem.at[at])
        for at in range(4)
    ]
    for load in own_loads:
        load.start()
    pl.semaphore_wait(barrier, n - 1)

    outputs = (second_out, first_out, value_out)

    def in_copy(at, peer, slot):
        return pltpu.make_async_remote_copy(
            src_ref=inputs[at].at[pl.ds(pl.multiple_of(peer * channels, channels), channels), :],
            dst_ref=recv.at[at, slot],
            send_sem=in_send.at[at, peer],
            recv_sem=in_recv.at[at, slot],
            device_id={"seq": peer},
            device_id_type=MESH,
        )

    def out_copy(at, peer, slot):
        return pltpu.make_async_remote_copy(
            src_ref=outs.at[at, peer],
            dst_ref=outputs[at].at[pl.ds(pl.multiple_of(slot * channels, channels), channels), :],
            send_sem=out_send.at[at, peer],
            recv_sem=out_recv.at[at, slot],
            device_id={"seq": peer},
            device_id_type=MESH,
        )

    def part_copy(peer, slot):
        return pltpu.make_async_remote_copy(
            src_ref=small_part.at[peer],
            dst_ref=small_recv.at[slot],
            send_sem=part_send.at[peer],
            recv_sem=part_recv.at[slot],
            device_id={"seq": peer},
            device_id_type=MESH,
        )

    def sum_copy(peer, slot):
        return pltpu.make_async_remote_copy(
            src_ref=small_sum,
            dst_ref=small_out.at[slot],
            send_sem=sum_send.at[peer],
            recv_sem=sum_recv.at[slot],
            device_id={"seq": peer},
            device_id_type=MESH,
        )

    def for_peers(action):
        def body(step, carry):
            action(lax.rem(me + step, n))
            return carry

        lax.fori_loop(1, n, body, 0)

    for at in range(4):
        for_peers(lambda peer, at=at: in_copy(at, peer, me).start())

    pos_table[...] = jnp.zeros_like(pos_table)
    for load in loads[:7]:
        load.wait()
    pos_table[0:features_used, :] = pos_weight_ref[...]
    pos_table[features_used : features_used + 1, :] = pos_bias_ref[...]
    features = features_ref[0:64, :]
    pre_one = split_dot(halves(pos_table[...]), (features, features_ref[64:128, :]))
    act_one, slope_one = sin_cos(pre_one)
    act_one = halves(act_one)
    mid_weight = mid_weight_ref[...]
    pre_two = split_dot(halves(mid_weight.T), act_one) + as_column(mid_bias_ref[...], 64)
    act_two, slope_two = sin_cos(pre_two)
    act_two = halves(act_two)

    def wanted(row):
        return jnp.where(row < channels, 2 * row, 2 * (row - channels) + 1) + 2 * channels * pair

    lane = lax.broadcasted_iota(jnp.int32, (2 * channels, 128), 1)
    row = lax.broadcasted_iota(jnp.int32, (2 * channels, 128), 0)
    rates_row = rates_ref[pl.ds(column, 1), :]
    own_rates = jnp.sum(jnp.where(lane == wanted(row), rates_row, 0.0), axis=1, keepdims=True)
    pick = lax.broadcasted_iota(jnp.int32, (128, 2 * channels), 0) == wanted(
        lax.broadcasted_iota(jnp.int32, (128, 2 * channels), 1)
    )
    pick = jnp.where(pick, 1.0, 0.0).astype(bf16)
    own_weight = tuple(
        short_dot(half, pick).astype(bf16) for half in halves(out_weight_ref[...])
    )
    ramp = lax.broadcasted_iota(jnp.int32, (1, seq_len), 1).astype(f32) * (1.0 / seq_len)
    window = jnp.exp(-own_rates * ramp)
    filters = (split_dot(own_weight, act_two) * window).astype(bf16)
    for load in loads[7:]:
        load.wait()

    def to_sections(rows):
        return jnp.concatenate(
            [
                jnp.concatenate(
                    [
                        rows[GROUP * g : GROUP * (g + 1), width * at : width * (at + 1)]
                        for at in range(n)
                    ],
                    axis=0,
                )
                for g in range(groups)
            ],
            axis=1,
        )

    def from_sections(data):
        return jnp.concatenate(
            [
                jnp.concatenate(
                    [
                        data[GROUP * at : GROUP * (at + 1), width * g : width * (g + 1)]
                        for at in range(n)
                    ],
                    axis=1,
                )
                for g in range(groups)
            ],
            axis=0,
        )

    def forward(data):
        stage = short_dot(left_fwd_ref[...], data)
        cos, sin = twid_cos_ref[...], twid_sin_ref[...]
        result = []
        for g in range(groups):
            real = stage[:rows_half, width * g : width * (g + 1)]
            imag = stage[rows_half:, width * g : width * (g + 1)]
            real_b = (real * cos + imag * sin).astype(bf16)
            imag_b = (imag * cos - real * sin).astype(bf16)
            spectrum = short_dot(jnp.concatenate([real_b, imag_b], axis=1), right_fwd_ref[...])
            result.append((spectrum[:, :width], spectrum[:, width:]))
        return result

    def inverse(left, right, conj_left, conj_right):
        cos, sin = twid_cos_ref[...], twid_sin_ref[...]
        sections = []
        for g in range(groups):
            real_p, imag_p = spectral_product(left[g], right[g], conj_left, conj_right)
            stage = short_dot(jnp.concatenate([real_p, imag_p], axis=1), right_inv_ref[...])
            real, imag = stage[:, :width], stage[:, width:]
            real_r = (real * cos - imag * sin).astype(bf16)
            imag_r = (imag * cos + real * sin).astype(bf16)
            sections.append(jnp.concatenate([real_r, imag_r], axis=0))
        return short_dot(left_inv_ref[...], jnp.concatenate(sections, axis=1))

    def arrived(at):
        own_loads[at].wait()
        for_peers(lambda peer: in_copy(at, peer, peer).wait_recv())
        return jnp.concatenate(
            [
                recv[at, :, GROUP * g : GROUP * (g + 1), :].reshape(half_rows, width)
                for g in range(groups)
            ],
            axis=1,
        )

    def send_out(at, data):
        for g in range(groups):
            outs[at, :, GROUP * g : GROUP * (g + 1), :] = data[
                :, width * g : width * (g + 1)
            ].reshape(n, GROUP, width)
        for_peers(lambda peer: out_copy(at, peer, me).start())
        outputs[at][own_rows, :] = outs[at, me]

    spec_one = forward(to_sections(filters[:channels]))
    spec_two = forward(to_sections(filters[channels:]))
    spec_val = forward(arrived(0))
    conv_one = inverse(spec_one, spec_val, False, False)
    first = arrived(1).astype(f32)
    spec_gated = forward((first * conv_one).astype(bf16))
    conv_two = inverse(spec_two, spec_gated, False, False)
    cot = arrived(2).astype(f32)
    send_out(0, (cot * conv_two).astype(bf16))
    second = arrived(3).astype(f32)
    spec_gtwo = forward((cot * second).astype(bf16))
    gated_grad = inverse(spec_two, spec_gtwo, True, False)
    send_out(1, (gated_grad * conv_one).astype(bf16))
    spec_gone = forward((gated_grad * first).astype(bf16))
    send_out(2, inverse(spec_one, spec_gone, True, False).astype(bf16))
    filt_one = from_sections(inverse(spec_gone, spec_val, False, True))
    filt_two = from_sections(inverse(spec_gtwo, spec_gated, False, True))
    filter_grad = jnp.concatenate([filt_one, filt_two], axis=0) * window * (1.0 / seq_len)

    filter_grad = filter_grad.astype(bf16)
    pre_two_grad = (short_dot(own_weight[0], filter_grad) * slope_two).astype(bf16)
    pre_one_grad = contract_dims(mid_weight.astype(bf16), pre_two_grad, 0, 0) * slope_one
    both = contract_dims(
        jnp.concatenate([pre_two_grad, pre_one_grad.astype(bf16)], axis=0),
        jnp.concatenate([act_one[0], features], axis=0),
        1,
        1,
    )
    lane = lax.broadcasted_iota(jnp.int32, (64, 128), 1)
    from_two = (lane < 64) | (lane == 64 + features_used + 1)
    small = jnp.where(from_two, both[:64], both[64:])
    share = small.shape[0] // n
    for at in range(n):
        small_part[at] = small[share * at : share * (at + 1), :]
    for_peers(lambda peer: part_copy(peer, me).start())
    small_recv[me] = small_part[me]

    weight_grad = contract_dims(filter_grad, act_two[0], 1, 1)
    for o in range(2):
        out_weight_out[pl.ds(o, channels, stride=2), :] = weight_grad[
            channels * o : channels * (o + 1)
        ]

    for_peers(lambda peer: part_copy(peer, peer).wait_recv())
    total = small_recv[0]
    for at in range(1, n):
        total = total + small_recv[at]
    small_sum[...] = total
    small_out[me] = total
    for_peers(lambda peer: sum_copy(peer, me).start())

    for at in range(4):
        for_peers(lambda peer, at=at: in_copy(at, peer, me).wait_send())
    for at in range(3):
        for_peers(lambda peer, at=at: out_copy(at, peer, me).wait_send())
        for_peers(lambda peer, at=at: out_copy(at, peer, peer).wait_recv())
    for_peers(lambda peer: part_copy(peer, me).wait_send())
    for_peers(lambda peer: sum_copy(peer, me).wait_send())
    for_peers(lambda peer: sum_copy(peer, peer).wait_recv())


def finish_kernel(
    features_used,
    value_in,
    first_in,
    second_in,
    weight_in,
    small_ref,
    value_out,
    first_out,
    second_out,
    weight_out,
    pos_weight_out,
    pos_bias_out,
    mid_weight_out,
    mid_bias_out,
    sem,
):
    copies = [
        pltpu.make_async_copy(source, target, sem.at[at])
        for at, (source, target) in enumerate(
            (
                (value_in, value_out),
                (first_in, first_out),
                (second_in, second_out),
                (weight_in, weight_out),
            )
        )
    ]
    for copy in copies:
        copy.start()
    small = small_ref[...]
    turned = small.T
    last = 64 + features_used
    pos_weight_out[...] = turned[64:last]
    pos_bias_out[...] = turned[last : last + 1]
    mid_bias_out[...] = turned[last + 1 : last + 2]
    mid_weight_out[...] = small[:, :64]
    for copy in copies:
        copy.wait()


def on_device(
    value_branch,
    first_gate,
    second_gate,
    out_cotangent,
    pos_weight,
    pos_bias,
    mid_weight,
    mid_bias,
    out_weight,
    decay_rates,
):
    model_width, tok_dev = value_branch.shape
    devices = lax.axis_size("seq")
    channels = model_width // devices
    hidden, features_used = pos_weight.shape
    fits = (
        tok_dev == RADIX
        and devices == 16
        and channels == 2 * GROUP
        and hidden == 64
        and features_used <= 61
        and out_weight.shape == (2 * model_width, 64)
    )
    if not fits:
        return on_device_plain(
            value_branch,
            first_gate,
            second_gate,
            out_cotangent,
            pos_weight,
            pos_bias,
            mid_weight,
            mid_bias,
            out_weight,
            decay_rates,
        )
    seq_len = tok_dev * devices
    freq_rows = 2 * devices
    tables = numpy_tables(freq_rows, RADIX, seq_len, (features_used - 1) // 2, GROUP)
    share = hidden // devices
    dma = pltpu.SemaphoreType.DMA
    vmem = pl.BlockSpec(memory_space=pltpu.VMEM)
    hbm = pl.BlockSpec(memory_space=pltpu.HBM)
    anywhere = pl.BlockSpec(memory_space=pl.ANY)
    bf16, f32 = jnp.bfloat16, jnp.float32
    value_out, first_out, second_out, weight_out, small = pl.pallas_call(
        functools.partial(operator_kernel, devices, channels, features_used),
        out_shape=[jax.ShapeDtypeStruct((model_width, tok_dev), jnp.bfloat16)] * 3
        + [
            jax.ShapeDtypeStruct((2 * channels, hidden), jnp.float32),
            jax.ShapeDtypeStruct((devices, share, 2 * hidden), jnp.float32),
        ],
        in_specs=[hbm] * 17,
        out_specs=[vmem] * 5,
        scratch_shapes=[
            pltpu.VMEM((4, devices, channels, RADIX), jnp.bfloat16),
            pltpu.VMEM((3, devices, channels, RADIX), jnp.bfloat16),
            pltpu.VMEM((devices, share, 2 * hidden), jnp.float32),
            pltpu.VMEM((devices, share, 2 * hidden), jnp.float32),
            pltpu.VMEM((share, 2 * hidden), jnp.float32),
            dma((4, devices)),
            dma((4, devices)),
            dma((3, devices)),
            dma((3, devices)),
            dma((devices,)),
            dma((devices,)),
            dma((devices,)),
            dma((devices,)),
            pltpu.VMEM((features_used, hidden), f32),
            pltpu.VMEM((1, hidden), f32),
            pltpu.VMEM((hidden, hidden), f32),
            pltpu.VMEM((1, hidden), f32),
            pltpu.VMEM((hidden, 128), f32),
            pltpu.VMEM((2 * model_width // 128, 128), f32),
            *[pltpu.VMEM(table.shape, table.dtype) for table in tables],
            pltpu.VMEM((hidden, hidden), f32),
            dma((13,)),
            dma((4,)),
        ],
        compiler_params=pltpu.CompilerParams(
            collective_id=0, has_side_effects=True, vmem_limit_bytes=50 * 1024 * 1024
        ),
    )(
        value_branch,
        first_gate,
        second_gate,
        out_cotangent,
        pos_weight.T,
        pos_bias.reshape(1, hidden),
        mid_weight,
        mid_bias.reshape(1, hidden),
        out_weight.T,
        decay_rates.reshape(2 * model_width // 128, 128),
        *[jnp.asarray(table) for table in tables],
    )
    small = small.reshape(hidden, 2 * hidden)
    shape = jax.ShapeDtypeStruct
    results = pl.pallas_call(
        functools.partial(finish_kernel, features_used),
        out_shape=[shape((model_width, tok_dev), bf16)] * 3
        + [
            shape((2 * channels, hidden), f32),
            shape((features_used, hidden), f32),
            shape((1, hidden), f32),
            shape((hidden, hidden), f32),
            shape((1, hidden), f32),
        ],
        in_specs=[anywhere] * 4 + [vmem],
        out_specs=[hbm] * 4 + [pl.BlockSpec()] * 4,
        scratch_shapes=[dma((4,))],
    )(value_out, first_out, second_out, weight_out, small)
    return (
        results[0],
        results[1],
        results[2],
        results[4].T,
        results[5].reshape(hidden),
        results[6],
        results[7].reshape(hidden),
        results[3],
    )


def solution(mesh):
    in_specs = (
        P(None, ("dp", "seq")),
        P(None, ("dp", "seq")),
        P(None, ("dp", "seq")),
        P(None, ("dp", "seq")),
        P(),
        P(),
        P(),
        P(),
        P(),
        P(),
    )
    out_specs = (
        P(None, ("dp", "seq")),
        P(None, ("dp", "seq")),
        P(None, ("dp", "seq")),
        P("dp", None),
        P("dp"),
        P("dp", None),
        P("dp"),
        P("seq", "dp"),
    )
    return jax.shard_map(
        on_device, mesh=mesh, in_specs=in_specs, out_specs=out_specs, check_vma=False
    )
```

```python
import functools
import math

import jax
import jax.numpy as jnp
import ml_dtypes
import numpy as np
from jax import lax
from jax.experimental import pallas as pl
from jax.experimental.pallas import tpu as pltpu
from jax.sharding import PartitionSpec as P

RADIX = 128
GROUP = 16
MESH = pl.DeviceIdType.MESH


def make_tables(freq_rows, radix):
    length_all = freq_rows * radix
    freq_index = jnp.arange(freq_rows, dtype=jnp.int32)
    half_index = jnp.arange(freq_rows // 2, dtype=jnp.int32)
    inner_index = jnp.arange(radix, dtype=jnp.int32)
    angle_one = (freq_index[:, None] * half_index[None, :] % freq_rows).astype(jnp.float32) * (
        2.0 * math.pi / freq_rows
    )
    angle_two = (inner_index[:, None] * inner_index[None, :] % radix).astype(jnp.float32) * (
        2.0 * math.pi / radix
    )
    angle_twid = (freq_index[:, None] * inner_index[None, :] % length_all).astype(jnp.float32) * (
        2.0 * math.pi / length_all
    )
    cos_one = jnp.cos(angle_one).astype(jnp.bfloat16)
    sin_one = jnp.sin(angle_one).astype(jnp.bfloat16)
    cos_two = jnp.cos(angle_two).astype(jnp.bfloat16)
    sin_two = jnp.sin(angle_two).astype(jnp.bfloat16)
    left_table = jnp.concatenate([cos_one, -sin_one], axis=0)
    right_fwd = jnp.concatenate(
        [jnp.concatenate([cos_two, -sin_two], axis=1), jnp.concatenate([sin_two, cos_two], axis=1)],
        axis=0,
    )
    right_inv = jnp.concatenate(
        [jnp.concatenate([cos_two, sin_two], axis=1), jnp.concatenate([-sin_two, cos_two], axis=1)],
        axis=0,
    )
    return (left_table, right_fwd, right_inv, jnp.cos(angle_twid), jnp.sin(angle_twid))


def forward_spectrum(signal, tables, freq_rows, radix):
    left_table, right_fwd, right_inv, twid_cos, twid_sin = tables
    count = signal.shape[0]
    shaped = signal.reshape(count, freq_rows // 2, radix)
    stacked = jnp.einsum("kn,rnm->rkm", left_table, shaped, preferred_element_type=jnp.float32)
    real_a = stacked[:, :freq_rows]
    imag_a = stacked[:, freq_rows:]
    real_b = (real_a * twid_cos + imag_a * twid_sin).astype(jnp.bfloat16)
    imag_b = (imag_a * twid_cos - real_a * twid_sin).astype(jnp.bfloat16)
    joined = jnp.concatenate([real_b, imag_b], axis=2)
    spectrum = jnp.einsum("rkn,nm->rkm", joined, right_fwd, preferred_element_type=jnp.float32)
    return (spectrum[:, :, :radix], spectrum[:, :, radix:])


def inverse_signal(product, tables, freq_rows, radix):
    left_table, right_fwd, right_inv, twid_cos, twid_sin = tables
    real_p, imag_p = product
    joined = jnp.concatenate([real_p, imag_p], axis=2)
    section_q = jnp.einsum("rkn,nm->rkm", joined, right_inv, preferred_element_type=jnp.float32)
    real_q = section_q[:, :, :radix]
    imag_q = section_q[:, :, radix:]
    real_r = (real_q * twid_cos - imag_q * twid_sin).astype(jnp.bfloat16)
    imag_r = (imag_q * twid_cos + real_q * twid_sin).astype(jnp.bfloat16)
    rows_both = jnp.concatenate([real_r, imag_r], axis=1)
    output = jnp.einsum("kn,rkm->rnm", left_table, rows_both, preferred_element_type=jnp.float32)
    count = real_p.shape[0]
    return (output * (1.0 / (freq_rows * radix))).reshape(count, freq_rows // 2 * radix)


def spectral_product(left, right, conj_left, conj_right):
    sign_left = -1.0 if conj_left else 1.0
    sign_right = -1.0 if conj_right else 1.0
    real_part = left[0] * right[0] - sign_left * sign_right * left[1] * right[1]
    imag_part = sign_left * left[1] * right[0] + sign_right * left[0] * right[1]
    return (real_part.astype(jnp.bfloat16), imag_part.astype(jnp.bfloat16))


def positional_features(positions, seq_len, bands):
    band_index = jnp.arange(1, bands + 1, dtype=jnp.int32)
    angles = (band_index[:, None] * positions[None, :] % seq_len).astype(jnp.float32) * (
        2.0 * math.pi / seq_len
    )
    ramp = positions.astype(jnp.float32)[None, :] / seq_len
    return jnp.concatenate([ramp, jnp.cos(angles), jnp.sin(angles)], axis=0)


def filter_network(positions, seq_len, pos_weight, pos_bias, mid_weight, mid_bias):
    bands = (pos_weight.shape[1] - 1) // 2
    features = positional_features(positions, seq_len, bands)
    pre_one = jnp.dot(pos_weight, features, precision=lax.Precision.HIGHEST) + pos_bias[:, None]
    act_one = jnp.sin(pre_one)
    pre_two = jnp.dot(mid_weight, act_one, precision=lax.Precision.HIGHEST) + mid_bias[:, None]
    act_two = jnp.sin(pre_two)
    return (features, pre_one, act_one, pre_two, act_two)


def modulation(rates, positions, seq_len):
    return jnp.exp(-rates[:, None] * positions.astype(jnp.float32)[None, :] / seq_len)


def contract_last(left, right):
    return lax.dot_general(left, right, (((1,), (1,)), ((), ())), precision=lax.Precision.HIGHEST)


def network_backward(act_grad, features, pre_one, act_one, pre_two, mid_weight):
    pre_two_grad = act_grad * jnp.cos(pre_two)
    mid_weight_part = contract_last(pre_two_grad, act_one)
    mid_bias_part = jnp.sum(pre_two_grad, axis=1)
    pre_one_grad = jnp.dot(mid_weight.T, pre_two_grad, precision=lax.Precision.HIGHEST) * jnp.cos(
        pre_one
    )
    pos_weight_part = contract_last(pre_one_grad, features)
    pos_bias_part = jnp.sum(pre_one_grad, axis=1)
    return (pos_weight_part, pos_bias_part, mid_weight_part, mid_bias_part)


def on_device_plain(
    value_branch,
    first_gate,
    second_gate,
    out_cotangent,
    pos_weight,
    pos_bias,
    mid_weight,
    mid_bias,
    out_weight,
    decay_rates,
):
    model_width, tok_dev = value_branch.shape
    devices = lax.axis_size("seq")
    seq_len = tok_dev * devices
    channels = model_width // devices
    my_rank = lax.axis_index("seq")
    freq_rows = 2 * seq_len // RADIX
    tables = make_tables(freq_rows, RADIX)
    all_positions = jnp.arange(seq_len, dtype=jnp.int32)
    own_rates = lax.dynamic_slice_in_dim(decay_rates, my_rank * 2 * channels, 2 * channels)
    window_own = modulation(own_rates, all_positions, seq_len)
    value_ch, first_ch = (
        lax.all_to_all(value_branch, "seq", split_axis=0, concat_axis=1, tiled=True),
        lax.all_to_all(first_gate, "seq", split_axis=0, concat_axis=1, tiled=True),
    )
    local_positions = my_rank * tok_dev + jnp.arange(tok_dev, dtype=jnp.int32)
    features, pre_one, act_one, pre_two, act_two = filter_network(
        local_positions, seq_len, pos_weight, pos_bias, mid_weight, mid_bias
    )
    window_local = modulation(decay_rates, local_positions, seq_len)
    local_filters = (
        jnp.dot(out_weight, act_two, precision=lax.Precision.HIGHEST) * window_local
    ).astype(jnp.bfloat16)
    filt_ch = lax.all_to_all(local_filters, "seq", split_axis=0, concat_axis=1, tiled=True)
    filt_real, filt_imag = forward_spectrum(filt_ch, tables, freq_rows, RADIX)
    filt_real = filt_real.reshape(channels, 2, freq_rows, RADIX)
    filt_imag = filt_imag.reshape(channels, 2, freq_rows, RADIX)
    spec_one = (filt_real[:, 0], filt_imag[:, 0])
    spec_two = (filt_real[:, 1], filt_imag[:, 1])
    spec_val = forward_spectrum(value_ch, tables, freq_rows, RADIX)
    conv_one = inverse_signal(
        spectral_product(spec_one, spec_val, False, False), tables, freq_rows, RADIX
    )
    gated = (first_ch.astype(jnp.float32) * conv_one).astype(jnp.bfloat16)
    spec_gated = forward_spectrum(gated, tables, freq_rows, RADIX)
    conv_two = inverse_signal(
        spectral_product(spec_two, spec_gated, False, False), tables, freq_rows, RADIX
    )
    second_ch, cot_ch = (
        lax.all_to_all(second_gate, "seq", split_axis=0, concat_axis=1, tiled=True),
        lax.all_to_all(out_cotangent, "seq", split_axis=0, concat_axis=1, tiled=True),
    )
    cot_wide = cot_ch.astype(jnp.float32)
    second_grad_ch = (cot_wide * conv_two).astype(jnp.bfloat16)
    second_out = lax.all_to_all(second_grad_ch, "seq", split_axis=1, concat_axis=0, tiled=True)
    grad_two = (cot_wide * second_ch.astype(jnp.float32)).astype(jnp.bfloat16)
    spec_gtwo = forward_spectrum(grad_two, tables, freq_rows, RADIX)
    gated_grad = inverse_signal(
        spectral_product(spec_two, spec_gtwo, True, False), tables, freq_rows, RADIX
    )
    filt_grad_two = inverse_signal(
        spectral_product(spec_gtwo, spec_gated, False, True), tables, freq_rows, RADIX
    )
    first_grad_ch = (gated_grad * conv_one).astype(jnp.bfloat16)
    grad_one = (gated_grad * first_ch.astype(jnp.float32)).astype(jnp.bfloat16)
    spec_gone = forward_spectrum(grad_one, tables, freq_rows, RADIX)
    value_grad_ch = inverse_signal(
        spectral_product(spec_one, spec_gone, True, False), tables, freq_rows, RADIX
    ).astype(jnp.bfloat16)
    filt_grad_one = inverse_signal(
        spectral_product(spec_gone, spec_val, False, True), tables, freq_rows, RADIX
    )
    value_out, first_out = (
        lax.all_to_all(value_grad_ch, "seq", split_axis=1, concat_axis=0, tiled=True),
        lax.all_to_all(first_grad_ch, "seq", split_axis=1, concat_axis=0, tiled=True),
    )
    filt_grads = jnp.stack([filt_grad_one, filt_grad_two], axis=1).reshape(2 * channels, seq_len)
    filter_grad_ch = filt_grads * window_own / seq_len
    filter_grad_seq = lax.all_to_all(
        filter_grad_ch.astype(jnp.bfloat16), "seq", split_axis=1, concat_axis=0, tiled=True
    ).astype(filter_grad_ch.dtype)
    out_weight_grad = lax.psum_scatter(
        contract_last(filter_grad_seq, act_two), "seq", scatter_dimension=0, tiled=True
    )
    act_grad = jnp.dot(out_weight.T, filter_grad_seq, precision=lax.Precision.HIGHEST)
    partials = network_backward(act_grad, features, pre_one, act_one, pre_two, mid_weight)
    pos_weight_grad, pos_bias_grad, mid_weight_grad, mid_bias_grad = lax.psum(
        (partials[0], partials[1], partials[2], partials[3]), "seq"
    )
    return (
        value_out,
        first_out,
        second_out,
        pos_weight_grad,
        pos_bias_grad,
        mid_weight_grad,
        mid_bias_grad,
        out_weight_grad,
    )


def numpy_tables(freq_rows, radix, seq_len, bands, group):
    half = freq_rows // 2
    length_all = freq_rows * radix
    freq_index = np.arange(freq_rows)
    inner = np.arange(radix)
    angle_one = (freq_index[:, None] * np.arange(half)[None, :] % freq_rows) * (2.0 * np.pi / freq_rows)
    angle_two = (inner[:, None] * inner[None, :] % radix) * (2.0 * np.pi / radix)
    angle_twid = (freq_index[:, None] * inner[None, :] % length_all) * (2.0 * np.pi / length_all)
    left = np.concatenate([np.cos(angle_one), -np.sin(angle_one)], axis=0)
    left_fwd = np.kron(left, np.eye(group))
    left_inv = left_fwd.T / length_all
    cos_two, sin_two = np.cos(angle_two), np.sin(angle_two)
    right_fwd = np.block([[cos_two, -sin_two], [sin_two, cos_two]])
    right_inv = np.block([[cos_two, sin_two], [-sin_two, cos_two]])
    twid_cos = np.repeat(np.cos(angle_twid), group, axis=0)
    twid_sin = np.repeat(np.sin(angle_twid), group, axis=0)
    positions = np.arange(seq_len)
    band = np.arange(1, bands + 1)
    angles = (band[:, None] * positions[None, :] % seq_len) * (2.0 * np.pi / seq_len)
    features = np.zeros((64, seq_len), np.float32)
    features[0] = positions / seq_len
    features[1 : bands + 1] = np.cos(angles)
    features[bands + 1 : 2 * bands + 1] = np.sin(angles)
    features[2 * bands + 1 : 2 * bands + 3] = 1.0
    upper = features.astype(ml_dtypes.bfloat16)
    lower = (features - upper.astype(np.float32)).astype(ml_dtypes.bfloat16)
    features = np.concatenate([upper, lower], axis=0)
    low = [table.astype(ml_dtypes.bfloat16) for table in (left_fwd, left_inv, right_fwd, right_inv)]
    wide = [table.astype(np.float32) for table in (twid_cos, twid_sin)]
    return low + wide + [features]


def sin_cos(x):
    turns = jnp.floor(x * (1.0 / math.pi) + 0.5)
    rest = x - turns * 3.140625
    rest = rest - turns * 9.67502593994140625e-4
    rest = rest - turns * 1.509957990978376432e-7
    sign = 1.0 - 2.0 * (turns - 2.0 * jnp.floor(turns * 0.5))
    square = rest * rest
    odd = 1.0 / 6227020800.0
    for term in (-1.0 / 39916800.0, 1.0 / 362880.0, -1.0 / 5040.0, 1.0 / 120.0, -1.0 / 6.0, 1.0):
        odd = odd * square + term
    even = 1.0 / 479001600.0
    for term in (-1.0 / 3628800.0, 1.0 / 40320.0, -1.0 / 720.0, 1.0 / 24.0, -0.5, 1.0):
        even = even * square + term
    return sign * rest * odd, sign * even


def short_dot(left, right):
    return jnp.dot(left, right, preferred_element_type=jnp.float32)


def contract_dims(left, right, left_dim, right_dim):
    return lax.dot_general(
        left, right, (((left_dim,), (right_dim,)), ((), ())), preferred_element_type=jnp.float32
    )


def halves(x):
    upper = x.astype(jnp.bfloat16)
    return upper, (x - upper.astype(jnp.float32)).astype(jnp.bfloat16)


def split_dot(left, right):
    return contract_dims(
        jnp.concatenate([left[0], left[1], left[0]], axis=0),
        jnp.concatenate([right[0], right[0], right[1]], axis=0),
        0,
        0,
    )


def as_column(row, count):
    width = row.shape[1]
    diagonal = lax.broadcasted_iota(jnp.int32, (count, width), 0) == lax.broadcasted_iota(
        jnp.int32, (count, width), 1
    )
    return jnp.sum(jnp.where(diagonal, row, 0.0), axis=1, keepdims=True)


def operator_kernel(
    devices,
    channels,
    features_used,
    value_ref,
    first_ref,
    second_ref,
    cot_ref,
    pos_weight_hbm,
    pos_bias_hbm,
    mid_weight_hbm,
    mid_bias_hbm,
    out_weight_hbm,
    rates_hbm,
    left_fwd_hbm,
    left_inv_hbm,
    right_fwd_hbm,
    right_inv_hbm,
    twid_cos_hbm,
    twid_sin_hbm,
    features_hbm,
    value_out,
    first_out,
    second_out,
    out_weight_out,
    small_out,
    recv,
    outs,
    small_part,
    small_recv,
    small_sum,
    in_send,
    in_recv,
    out_send,
    out_recv,
    part_send,
    part_recv,
    sum_send,
    sum_recv,
    pos_weight_ref,
    pos_bias_ref,
    mid_weight_ref,
    mid_bias_ref,
    out_weight_ref,
    rates_ref,
    left_fwd_ref,
    left_inv_ref,
    right_fwd_ref,
    right_inv_ref,
    twid_cos_ref,
    twid_sin_ref,
    features_ref,
    pos_table,
    load_sem,
    own_sem,
):
    n = devices
    me = lax.axis_index("seq")
    width = RADIX
    seq_len = n * width
    groups = channels // GROUP
    rows_half = 2 * n * GROUP
    half_rows = n * GROUP
    bf16 = jnp.bfloat16
    f32 = jnp.float32

    barrier = pltpu.get_barrier_semaphore()

    def greet(step, carry):
        pl.semaphore_signal(
            barrier, inc=1, device_id={"seq": lax.rem(me + step, n)}, device_id_type=MESH
        )
        return carry

    lax.fori_loop(1, n, greet, 0)

    inputs = (value_ref, first_ref, cot_ref, second_ref)
    own_rows = pl.ds(pl.multiple_of(me * channels, channels), channels)
    pair = lax.rem(me, 2)
    column = me // 2
    loads = [
        pltpu.make_async_copy(source, target, load_sem.at[at])
        for at, (source, target) in enumerate(
            (
                (pos_weight_hbm, pos_weight_ref),
                (pos_bias_hbm, pos_bias_ref),
                (features_hbm, features_ref),
                (mid_weight_hbm, mid_weight_ref),
                (mid_bias_hbm, mid_bias_ref),
                (out_weight_hbm.at[:, pl.ds(pl.multiple_of(column * 128, 128), 128)], out_weight_ref),
                (rates_hbm, rates_ref),
                (left_fwd_hbm, left_fwd_ref),
                (right_fwd_hbm, right_fwd_ref),
                (twid_cos_hbm, twid_cos_ref),
                (twid_sin_hbm, twid_sin_ref),
                (right_inv_hbm, right_inv_ref),
                (left_inv_hbm, left_inv_ref),
            )
        )
    ]
    for load in loads:
        load.start()
    own_loads = [
        pltpu.make_async_copy(inputs[at].at[own_rows, :], recv.at[at, me], own_sem.at[at])
        for at in range(4)
    ]
    for load in own_loads:
        load.start()
    pl.semaphore_wait(barrier, n - 1)

    outputs = (second_out, first_out, value_out)

    def in_copy(at, peer, slot):
        return pltpu.make_async_remote_copy(
            src_ref=inputs[at].at[pl.ds(pl.multiple_of(peer * channels, channels), channels), :],
            dst_ref=recv.at[at, slot],
            send_sem=in_send.at[at, peer],
            recv_sem=in_recv.at[at, slot],
            device_id={"seq": peer},
            device_id_type=MESH,
        )

    def out_copy(at, peer, slot):
        return pltpu.make_async_remote_copy(
            src_ref=outs.at[at, peer],
            dst_ref=outputs[at].at[pl.ds(pl.multiple_of(slot * channels, channels), channels), :],
            send_sem=out_send.at[at, peer],
            recv_sem=out_recv.at[at, slot],
            device_id={"seq": peer},
            device_id_type=MESH,
        )

    def part_copy(peer, slot):
        return pltpu.make_async_remote_copy(
            src_ref=small_part.at[peer],
            dst_ref=small_recv.at[slot],
            send_sem=part_send.at[peer],
            recv_sem=part_recv.at[slot],
            device_id={"seq": peer},
            device_id_type=MESH,
        )

    def sum_copy(peer, slot):
        return pltpu.make_async_remote_copy(
            src_ref=small_sum,
            dst_ref=small_out.at[slot],
            send_sem=sum_send.at[peer],
            recv_sem=sum_recv.at[slot],
            device_id={"seq": peer},
            device_id_type=MESH,
        )

    def for_peers(action):
        def body(step, carry):
            action(lax.rem(me + step, n))
            return carry

        lax.fori_loop(1, n, body, 0)

    for at in range(4):
        for_peers(lambda peer, at=at: in_copy(at, peer, me).start())

    pos_table[...] = jnp.zeros_like(pos_table)
    for load in loads[:7]:
        load.wait()
    pos_table[0:features_used, :] = pos_weight_ref[...]
    pos_table[features_used : features_used + 1, :] = pos_bias_ref[...]
    features = features_ref[0:64, :]
    pre_one = split_dot(halves(pos_table[...]), (features, features_ref[64:128, :]))
    act_one, slope_one = sin_cos(pre_one)
    act_one = halves(act_one)
    mid_weight = mid_weight_ref[...]
    pre_two = split_dot(halves(mid_weight.T), act_one) + as_column(mid_bias_ref[...], 64)
    act_two, slope_two = sin_cos(pre_two)
    act_two = halves(act_two)

    def wanted(row):
        return jnp.where(row < channels, 2 * row, 2 * (row - channels) + 1) + 2 * channels * pair

    lane = lax.broadcasted_iota(jnp.int32, (2 * channels, 128), 1)
    row = lax.broadcasted_iota(jnp.int32, (2 * channels, 128), 0)
    rates_row = rates_ref[pl.ds(column, 1), :]
    own_rates = jnp.sum(jnp.where(lane == wanted(row), rates_row, 0.0), axis=1, keepdims=True)
    pick = lax.broadcasted_iota(jnp.int32, (128, 2 * channels), 0) == wanted(
        lax.broadcasted_iota(jnp.int32, (128, 2 * channels), 1)
    )
    pick = jnp.where(pick, 1.0, 0.0).astype(bf16)
    own_weight = tuple(
        short_dot(half, pick).astype(bf16) for half in halves(out_weight_ref[...])
    )
    ramp = lax.broadcasted_iota(jnp.int32, (1, seq_len), 1).astype(f32) * (1.0 / seq_len)
    window = jnp.exp(-own_rates * ramp)
    filters = (split_dot(own_weight, act_two) * window).astype(bf16)
    for load in loads[7:]:
        load.wait()

    def to_sections(rows):
        return jnp.concatenate(
            [
                jnp.concatenate(
                    [
                        rows[GROUP * g : GROUP * (g + 1), width * at : width * (at + 1)]
                        for at in range(n)
                    ],
                    axis=0,
                )
                for g in range(groups)
            ],
            axis=1,
        )

    def from_sections(data):
        return jnp.concatenate(
            [
                jnp.concatenate(
                    [
                        data[GROUP * at : GROUP * (at + 1), width * g : width * (g + 1)]
                        for at in range(n)
                    ],
                    axis=1,
                )
                for g in range(groups)
            ],
            axis=0,
        )

    def forward(data):
        stage = short_dot(left_fwd_ref[...], data)
        cos, sin = twid_cos_ref[...], twid_sin_ref[...]
        result = []
        for g in range(groups):
            real = stage[:rows_half, width * g : width * (g + 1)]
            imag = stage[rows_half:, width * g : width * (g + 1)]
            real_b = (real * cos + imag * sin).astype(bf16)
            imag_b = (imag * cos - real * sin).astype(bf16)
            spectrum = short_dot(jnp.concatenate([real_b, imag_b], axis=1), right_fwd_ref[...])
            result.append((spectrum[:, :width], spectrum[:, width:]))
        return result

    def inverse(left, right, conj_left, conj_right):
        cos, sin = twid_cos_ref[...], twid_sin_ref[...]
        sections = []
        for g in range(groups):
            real_p, imag_p = spectral_product(left[g], right[g], conj_left, conj_right)
            stage = short_dot(jnp.concatenate([real_p, imag_p], axis=1), right_inv_ref[...])
            real, imag = stage[:, :width], stage[:, width:]
            real_r = (real * cos - imag * sin).astype(bf16)
            imag_r = (imag * cos + real * sin).astype(bf16)
            sections.append(jnp.concatenate([real_r, imag_r], axis=0))
        return short_dot(left_inv_ref[...], jnp.concatenate(sections, axis=1))

    def arrived(at):
        own_loads[at].wait()
        for_peers(lambda peer: in_copy(at, peer, peer).wait_recv())
        return jnp.concatenate(
            [
                recv[at, :, GROUP * g : GROUP * (g + 1), :].reshape(half_rows, width)
                for g in range(groups)
            ],
            axis=1,
        )

    def send_out(at, data):
        for g in range(groups):
            outs[at, :, GROUP * g : GROUP * (g + 1), :] = data[
                :, width * g : width * (g + 1)
            ].reshape(n, GROUP, width)
        for_peers(lambda peer: out_copy(at, peer, me).start())
        outputs[at][own_rows, :] = outs[at, me]

    spec_one = forward(to_sections(filters[:channels]))
    spec_two = forward(to_sections(filters[channels:]))
    spec_val = forward(arrived(0))
    conv_one = inverse(spec_one, spec_val, False, False)
    first = arrived(1).astype(f32)
    spec_gated = forward((first * conv_one).astype(bf16))
    conv_two = inverse(spec_two, spec_gated, False, False)
    cot = arrived(2).astype(f32)
    send_out(0, (cot * conv_two).astype(bf16))
    second = arrived(3).astype(f32)
    spec_gtwo = forward((cot * second).astype(bf16))
    gated_grad = inverse(spec_two, spec_gtwo, True, False)
    send_out(1, (gated_grad * conv_one).astype(bf16))
    spec_gone = forward((gated_grad * first).astype(bf16))
    send_out(2, inverse(spec_one, spec_gone, True, False).astype(bf16))
    filt_one = from_sections(inverse(spec_gone, spec_val, False, True))
    filt_two = from_sections(inverse(spec_gtwo, spec_gated, False, True))
    filter_grad = jnp.concatenate([filt_one, filt_two], axis=0) * window * (1.0 / seq_len)

    filter_grad = filter_grad.astype(bf16)
    pre_two_grad = (short_dot(own_weight[0], filter_grad) * slope_two).astype(bf16)
    pre_one_grad = contract_dims(mid_weight.astype(bf16), pre_two_grad, 0, 0) * slope_one
    both = contract_dims(
        jnp.concatenate([pre_two_grad, pre_one_grad.astype(bf16)], axis=0),
        jnp.concatenate([act_one[0], features], axis=0),
        1,
        1,
    )
    lane = lax.broadcasted_iota(jnp.int32, (64, 128), 1)
    from_two = (lane < 64) | (lane == 64 + features_used + 1)
    small = jnp.where(from_two, both[:64], both[64:])
    share = small.shape[0] // n
    for at in range(n):
        small_part[at] = small[share * at : share * (at + 1), :]
    for_peers(lambda peer: part_copy(peer, me).start())
    small_recv[me] = small_part[me]

    weight_grad = contract_dims(filter_grad, act_two[0], 1, 1)
    for o in range(2):
        out_weight_out[pl.ds(o, channels, stride=2), :] = weight_grad[
            channels * o : channels * (o + 1)
        ]

    for_peers(lambda peer: part_copy(peer, peer).wait_recv())
    total = small_recv[0]
    for at in range(1, n):
        total = total + small_recv[at]
    small_sum[...] = total
    small_out[me] = total
    for_peers(lambda peer: sum_copy(peer, me).start())

    for at in range(4):
        for_peers(lambda peer, at=at: in_copy(at, peer, me).wait_send())
    for at in range(3):
        for_peers(lambda peer, at=at: out_copy(at, peer, me).wait_send())
        for_peers(lambda peer, at=at: out_copy(at, peer, peer).wait_recv())
    for_peers(lambda peer: part_copy(peer, me).wait_send())
    for_peers(lambda peer: sum_copy(peer, me).wait_send())
    for_peers(lambda peer: sum_copy(peer, peer).wait_recv())


def finish_kernel(
    features_used,
    value_in,
    first_in,
    second_in,
    weight_in,
    small_in,
    value_out,
    first_out,
    second_out,
    weight_out,
    pos_weight_out,
    pos_bias_out,
    mid_weight_out,
    mid_bias_out,
    value_ref,
    first_ref,
    second_ref,
    weight_ref,
    small_ref,
    in_sem,
    out_sem,
):
    sources = (small_in, value_in, first_in, second_in, weight_in)
    held = (small_ref, value_ref, first_ref, second_ref, weight_ref)
    targets = (None, value_out, first_out, second_out, weight_out)
    loads = [
        pltpu.make_async_copy(sources[at], held[at], in_sem.at[at]) for at in range(5)
    ]
    stores = [
        pltpu.make_async_copy(held[at], targets[at], out_sem.at[at]) for at in range(1, 5)
    ]
    for load in loads:
        load.start()
    for load, store in zip(loads[1:], stores):
        load.wait()
        store.start()
    loads[0].wait()
    small = small_ref[...]
    turned = small.T
    last = 64 + features_used
    pos_weight_out[...] = turned[64:last]
    pos_bias_out[...] = turned[last : last + 1]
    mid_bias_out[...] = turned[last + 1 : last + 2]
    mid_weight_out[...] = small[:, :64]
    for store in stores:
        store.wait()


def on_device(
    value_branch,
    first_gate,
    second_gate,
    out_cotangent,
    pos_weight,
    pos_bias,
    mid_weight,
    mid_bias,
    out_weight,
    decay_rates,
):
    model_width, tok_dev = value_branch.shape
    devices = lax.axis_size("seq")
    channels = model_width // devices
    hidden, features_used = pos_weight.shape
    fits = (
        tok_dev == RADIX
        and devices == 16
        and channels == 2 * GROUP
        and hidden == 64
        and features_used <= 61
        and out_weight.shape == (2 * model_width, 64)
    )
    if not fits:
        return on_device_plain(
            value_branch,
            first_gate,
            second_gate,
            out_cotangent,
            pos_weight,
            pos_bias,
            mid_weight,
            mid_bias,
            out_weight,
            decay_rates,
        )
    seq_len = tok_dev * devices
    freq_rows = 2 * devices
    tables = numpy_tables(freq_rows, RADIX, seq_len, (features_used - 1) // 2, GROUP)
    share = hidden // devices
    dma = pltpu.SemaphoreType.DMA
    vmem = pl.BlockSpec(memory_space=pltpu.VMEM)
    hbm = pl.BlockSpec(memory_space=pltpu.HBM)
    bf16, f32 = jnp.bfloat16, jnp.float32
    value_out, first_out, second_out, weight_out, small = pl.pallas_call(
        functools.partial(operator_kernel, devices, channels, features_used),
        out_shape=[jax.ShapeDtypeStruct((model_width, tok_dev), jnp.bfloat16)] * 3
        + [
            jax.ShapeDtypeStruct((2 * channels, hidden), jnp.float32),
            jax.ShapeDtypeStruct((devices, share, 2 * hidden), jnp.float32),
        ],
        in_specs=[hbm] * 17,
        out_specs=[vmem] * 5,
        scratch_shapes=[
            pltpu.VMEM((4, devices, channels, RADIX), jnp.bfloat16),
            pltpu.VMEM((3, devices, channels, RADIX), jnp.bfloat16),
            pltpu.VMEM((devices, share, 2 * hidden), jnp.float32),
            pltpu.VMEM((devices, share, 2 * hidden), jnp.float32),
            pltpu.VMEM((share, 2 * hidden), jnp.float32),
            dma((4, devices)),
            dma((4, devices)),
            dma((3, devices)),
            dma((3, devices)),
            dma((devices,)),
            dma((devices,)),
            dma((devices,)),
            dma((devices,)),
            pltpu.VMEM((features_used, hidden), f32),
            pltpu.VMEM((1, hidden), f32),
            pltpu.VMEM((hidden, hidden), f32),
            pltpu.VMEM((1, hidden), f32),
            pltpu.VMEM((hidden, 128), f32),
            pltpu.VMEM((2 * model_width // 128, 128), f32),
            *[pltpu.VMEM(table.shape, table.dtype) for table in tables],
            pltpu.VMEM((hidden, hidden), f32),
            dma((13,)),
            dma((4,)),
        ],
        compiler_params=pltpu.CompilerParams(
            collective_id=0, has_side_effects=True, vmem_limit_bytes=62 * 1024 * 1024
        ),
    )(
        value_branch,
        first_gate,
        second_gate,
        out_cotangent,
        pos_weight.T,
        pos_bias.reshape(1, hidden),
        mid_weight,
        mid_bias.reshape(1, hidden),
        out_weight.T,
        decay_rates.reshape(2 * model_width // 128, 128),
        *[jnp.asarray(table) for table in tables],
    )
    small = small.reshape(hidden, 2 * hidden)
    shape = jax.ShapeDtypeStruct
    results = pl.pallas_call(
        functools.partial(finish_kernel, features_used),
        out_shape=[shape((model_width, tok_dev), bf16)] * 3
        + [
            shape((2 * channels, hidden), f32),
            shape((features_used, hidden), f32),
            shape((1, hidden), f32),
            shape((hidden, hidden), f32),
            shape((1, hidden), f32),
        ],
        in_specs=[hbm] * 5,
        out_specs=[hbm] * 4 + [pl.BlockSpec()] * 4,
        scratch_shapes=[pltpu.VMEM((model_width, tok_dev), bf16)] * 3
        + [
            pltpu.VMEM((2 * channels, hidden), f32),
            pltpu.VMEM((hidden, 2 * hidden), f32),
            dma((5,)),
            dma((5,)),
        ],
        compiler_params=pltpu.CompilerParams(vmem_limit_bytes=62 * 1024 * 1024),
    )(value_out, first_out, second_out, weight_out, small)
    return (
        results[0],
        results[1],
        results[2],
        results[4].T,
        results[5].reshape(hidden),
        results[6],
        results[7].reshape(hidden),
        results[3],
    )


def solution(mesh):
    in_specs = (
        P(None, ("dp", "seq")),
        P(None, ("dp", "seq")),
        P(None, ("dp", "seq")),
        P(None, ("dp", "seq")),
        P(),
        P(),
        P(),
        P(),
        P(),
        P(),
    )
    out_specs = (
        P(None, ("dp", "seq")),
        P(None, ("dp", "seq")),
        P(None, ("dp", "seq")),
        P("dp", None),
        P("dp"),
        P("dp", None),
        P("dp"),
        P("seq", "dp"),
    )
    return jax.shard_map(
        on_device, mesh=mesh, in_specs=in_specs, out_specs=out_specs, check_vma=False
    )
```

```python
import functools
import math

import jax
import jax.numpy as jnp
import ml_dtypes
import numpy as np
from jax import lax
from jax.experimental import pallas as pl
from jax.experimental.pallas import tpu as pltpu
from jax.sharding import PartitionSpec as P

RADIX = 128
GROUP = 16
MESH = pl.DeviceIdType.MESH


def make_tables(freq_rows, radix):
    length_all = freq_rows * radix
    freq_index = jnp.arange(freq_rows, dtype=jnp.int32)
    half_index = jnp.arange(freq_rows // 2, dtype=jnp.int32)
    inner_index = jnp.arange(radix, dtype=jnp.int32)
    angle_one = (freq_index[:, None] * half_index[None, :] % freq_rows).astype(jnp.float32) * (
        2.0 * math.pi / freq_rows
    )
    angle_two = (inner_index[:, None] * inner_index[None, :] % radix).astype(jnp.float32) * (
        2.0 * math.pi / radix
    )
    angle_twid = (freq_index[:, None] * inner_index[None, :] % length_all).astype(jnp.float32) * (
        2.0 * math.pi / length_all
    )
    cos_one = jnp.cos(angle_one).astype(jnp.bfloat16)
    sin_one = jnp.sin(angle_one).astype(jnp.bfloat16)
    cos_two = jnp.cos(angle_two).astype(jnp.bfloat16)
    sin_two = jnp.sin(angle_two).astype(jnp.bfloat16)
    left_table = jnp.concatenate([cos_one, -sin_one], axis=0)
    right_fwd = jnp.concatenate(
        [jnp.concatenate([cos_two, -sin_two], axis=1), jnp.concatenate([sin_two, cos_two], axis=1)],
        axis=0,
    )
    right_inv = jnp.concatenate(
        [jnp.concatenate([cos_two, sin_two], axis=1), jnp.concatenate([-sin_two, cos_two], axis=1)],
        axis=0,
    )
    return (left_table, right_fwd, right_inv, jnp.cos(angle_twid), jnp.sin(angle_twid))


def forward_spectrum(signal, tables, freq_rows, radix):
    left_table, right_fwd, right_inv, twid_cos, twid_sin = tables
    count = signal.shape[0]
    shaped = signal.reshape(count, freq_rows // 2, radix)
    stacked = jnp.einsum("kn,rnm->rkm", left_table, shaped, preferred_element_type=jnp.float32)
    real_a = stacked[:, :freq_rows]
    imag_a = stacked[:, freq_rows:]
    real_b = (real_a * twid_cos + imag_a * twid_sin).astype(jnp.bfloat16)
    imag_b = (imag_a * twid_cos - real_a * twid_sin).astype(jnp.bfloat16)
    joined = jnp.concatenate([real_b, imag_b], axis=2)
    spectrum = jnp.einsum("rkn,nm->rkm", joined, right_fwd, preferred_element_type=jnp.float32)
    return (spectrum[:, :, :radix], spectrum[:, :, radix:])


def inverse_signal(product, tables, freq_rows, radix):
    left_table, right_fwd, right_inv, twid_cos, twid_sin = tables
    real_p, imag_p = product
    joined = jnp.concatenate([real_p, imag_p], axis=2)
    section_q = jnp.einsum("rkn,nm->rkm", joined, right_inv, preferred_element_type=jnp.float32)
    real_q = section_q[:, :, :radix]
    imag_q = section_q[:, :, radix:]
    real_r = (real_q * twid_cos - imag_q * twid_sin).astype(jnp.bfloat16)
    imag_r = (imag_q * twid_cos + real_q * twid_sin).astype(jnp.bfloat16)
    rows_both = jnp.concatenate([real_r, imag_r], axis=1)
    output = jnp.einsum("kn,rkm->rnm", left_table, rows_both, preferred_element_type=jnp.float32)
    count = real_p.shape[0]
    return (output * (1.0 / (freq_rows * radix))).reshape(count, freq_rows // 2 * radix)


def spectral_product(left, right, conj_left, conj_right):
    sign_left = -1.0 if conj_left else 1.0
    sign_right = -1.0 if conj_right else 1.0
    real_part = left[0] * right[0] - sign_left * sign_right * left[1] * right[1]
    imag_part = sign_left * left[1] * right[0] + sign_right * left[0] * right[1]
    return (real_part.astype(jnp.bfloat16), imag_part.astype(jnp.bfloat16))


def positional_features(positions, seq_len, bands):
    band_index = jnp.arange(1, bands + 1, dtype=jnp.int32)
    angles = (band_index[:, None] * positions[None, :] % seq_len).astype(jnp.float32) * (
        2.0 * math.pi / seq_len
    )
    ramp = positions.astype(jnp.float32)[None, :] / seq_len
    return jnp.concatenate([ramp, jnp.cos(angles), jnp.sin(angles)], axis=0)


def filter_network(positions, seq_len, pos_weight, pos_bias, mid_weight, mid_bias):
    bands = (pos_weight.shape[1] - 1) // 2
    features = positional_features(positions, seq_len, bands)
    pre_one = jnp.dot(pos_weight, features, precision=lax.Precision.HIGHEST) + pos_bias[:, None]
    act_one = jnp.sin(pre_one)
    pre_two = jnp.dot(mid_weight, act_one, precision=lax.Precision.HIGHEST) + mid_bias[:, None]
    act_two = jnp.sin(pre_two)
    return (features, pre_one, act_one, pre_two, act_two)


def modulation(rates, positions, seq_len):
    return jnp.exp(-rates[:, None] * positions.astype(jnp.float32)[None, :] / seq_len)


def contract_last(left, right):
    return lax.dot_general(left, right, (((1,), (1,)), ((), ())), precision=lax.Precision.HIGHEST)


def network_backward(act_grad, features, pre_one, act_one, pre_two, mid_weight):
    pre_two_grad = act_grad * jnp.cos(pre_two)
    mid_weight_part = contract_last(pre_two_grad, act_one)
    mid_bias_part = jnp.sum(pre_two_grad, axis=1)
    pre_one_grad = jnp.dot(mid_weight.T, pre_two_grad, precision=lax.Precision.HIGHEST) * jnp.cos(
        pre_one
    )
    pos_weight_part = contract_last(pre_one_grad, features)
    pos_bias_part = jnp.sum(pre_one_grad, axis=1)
    return (pos_weight_part, pos_bias_part, mid_weight_part, mid_bias_part)


def on_device_plain(
    value_branch,
    first_gate,
    second_gate,
    out_cotangent,
    pos_weight,
    pos_bias,
    mid_weight,
    mid_bias,
    out_weight,
    decay_rates,
):
    model_width, tok_dev = value_branch.shape
    devices = lax.axis_size("seq")
    seq_len = tok_dev * devices
    channels = model_width // devices
    my_rank = lax.axis_index("seq")
    freq_rows = 2 * seq_len // RADIX
    tables = make_tables(freq_rows, RADIX)
    all_positions = jnp.arange(seq_len, dtype=jnp.int32)
    own_rates = lax.dynamic_slice_in_dim(decay_rates, my_rank * 2 * channels, 2 * channels)
    window_own = modulation(own_rates, all_positions, seq_len)
    value_ch, first_ch = (
        lax.all_to_all(value_branch, "seq", split_axis=0, concat_axis=1, tiled=True),
        lax.all_to_all(first_gate, "seq", split_axis=0, concat_axis=1, tiled=True),
    )
    local_positions = my_rank * tok_dev + jnp.arange(tok_dev, dtype=jnp.int32)
    features, pre_one, act_one, pre_two, act_two = filter_network(
        local_positions, seq_len, pos_weight, pos_bias, mid_weight, mid_bias
    )
    window_local = modulation(decay_rates, local_positions, seq_len)
    local_filters = (
        jnp.dot(out_weight, act_two, precision=lax.Precision.HIGHEST) * window_local
    ).astype(jnp.bfloat16)
    filt_ch = lax.all_to_all(local_filters, "seq", split_axis=0, concat_axis=1, tiled=True)
    filt_real, filt_imag = forward_spectrum(filt_ch, tables, freq_rows, RADIX)
    filt_real = filt_real.reshape(channels, 2, freq_rows, RADIX)
    filt_imag = filt_imag.reshape(channels, 2, freq_rows, RADIX)
    spec_one = (filt_real[:, 0], filt_imag[:, 0])
    spec_two = (filt_real[:, 1], filt_imag[:, 1])
    spec_val = forward_spectrum(value_ch, tables, freq_rows, RADIX)
    conv_one = inverse_signal(
        spectral_product(spec_one, spec_val, False, False), tables, freq_rows, RADIX
    )
    gated = (first_ch.astype(jnp.float32) * conv_one).astype(jnp.bfloat16)
    spec_gated = forward_spectrum(gated, tables, freq_rows, RADIX)
    conv_two = inverse_signal(
        spectral_product(spec_two, spec_gated, False, False), tables, freq_rows, RADIX
    )
    second_ch, cot_ch = (
        lax.all_to_all(second_gate, "seq", split_axis=0, concat_axis=1, tiled=True),
        lax.all_to_all(out_cotangent, "seq", split_axis=0, concat_axis=1, tiled=True),
    )
    cot_wide = cot_ch.astype(jnp.float32)
    second_grad_ch = (cot_wide * conv_two).astype(jnp.bfloat16)
    second_out = lax.all_to_all(second_grad_ch, "seq", split_axis=1, concat_axis=0, tiled=True)
    grad_two = (cot_wide * second_ch.astype(jnp.float32)).astype(jnp.bfloat16)
    spec_gtwo = forward_spectrum(grad_two, tables, freq_rows, RADIX)
    gated_grad = inverse_signal(
        spectral_product(spec_two, spec_gtwo, True, False), tables, freq_rows, RADIX
    )
    filt_grad_two = inverse_signal(
        spectral_product(spec_gtwo, spec_gated, False, True), tables, freq_rows, RADIX
    )
    first_grad_ch = (gated_grad * conv_one).astype(jnp.bfloat16)
    grad_one = (gated_grad * first_ch.astype(jnp.float32)).astype(jnp.bfloat16)
    spec_gone = forward_spectrum(grad_one, tables, freq_rows, RADIX)
    value_grad_ch = inverse_signal(
        spectral_product(spec_one, spec_gone, True, False), tables, freq_rows, RADIX
    ).astype(jnp.bfloat16)
    filt_grad_one = inverse_signal(
        spectral_product(spec_gone, spec_val, False, True), tables, freq_rows, RADIX
    )
    value_out, first_out = (
        lax.all_to_all(value_grad_ch, "seq", split_axis=1, concat_axis=0, tiled=True),
        lax.all_to_all(first_grad_ch, "seq", split_axis=1, concat_axis=0, tiled=True),
    )
    filt_grads = jnp.stack([filt_grad_one, filt_grad_two], axis=1).reshape(2 * channels, seq_len)
    filter_grad_ch = filt_grads * window_own / seq_len
    filter_grad_seq = lax.all_to_all(
        filter_grad_ch.astype(jnp.bfloat16), "seq", split_axis=1, concat_axis=0, tiled=True
    ).astype(filter_grad_ch.dtype)
    out_weight_grad = lax.psum_scatter(
        contract_last(filter_grad_seq, act_two), "seq", scatter_dimension=0, tiled=True
    )
    act_grad = jnp.dot(out_weight.T, filter_grad_seq, precision=lax.Precision.HIGHEST)
    partials = network_backward(act_grad, features, pre_one, act_one, pre_two, mid_weight)
    pos_weight_grad, pos_bias_grad, mid_weight_grad, mid_bias_grad = lax.psum(
        (partials[0], partials[1], partials[2], partials[3]), "seq"
    )
    return (
        value_out,
        first_out,
        second_out,
        pos_weight_grad,
        pos_bias_grad,
        mid_weight_grad,
        mid_bias_grad,
        out_weight_grad,
    )


def numpy_tables(freq_rows, radix, seq_len, bands, group):
    half = freq_rows // 2
    length_all = freq_rows * radix
    freq_index = np.arange(freq_rows)
    inner = np.arange(radix)
    angle_one = (freq_index[:, None] * np.arange(half)[None, :] % freq_rows) * (2.0 * np.pi / freq_rows)
    angle_two = (inner[:, None] * inner[None, :] % radix) * (2.0 * np.pi / radix)
    angle_twid = (freq_index[:, None] * inner[None, :] % length_all) * (2.0 * np.pi / length_all)
    left = np.concatenate([np.cos(angle_one), -np.sin(angle_one)], axis=0)
    left_fwd = np.kron(left, np.eye(group))
    left_inv = left_fwd.T / length_all
    cos_two, sin_two = np.cos(angle_two), np.sin(angle_two)
    right_fwd = np.block([[cos_two, -sin_two], [sin_two, cos_two]])
    right_inv = np.block([[cos_two, sin_two], [-sin_two, cos_two]])
    twid_cos = np.repeat(np.cos(angle_twid), group, axis=0)
    twid_sin = np.repeat(np.sin(angle_twid), group, axis=0)
    positions = np.arange(seq_len)
    band = np.arange(1, bands + 1)
    angles = (band[:, None] * positions[None, :] % seq_len) * (2.0 * np.pi / seq_len)
    features = np.zeros((64, seq_len), np.float32)
    features[0] = positions / seq_len
    features[1 : bands + 1] = np.cos(angles)
    features[bands + 1 : 2 * bands + 1] = np.sin(angles)
    features[2 * bands + 1 : 2 * bands + 3] = 1.0
    upper = features.astype(ml_dtypes.bfloat16)
    lower = (features - upper.astype(np.float32)).astype(ml_dtypes.bfloat16)
    features = np.concatenate([upper, lower], axis=0)
    low = [table.astype(ml_dtypes.bfloat16) for table in (left_fwd, left_inv, right_fwd, right_inv)]
    wide = [table.astype(np.float32) for table in (twid_cos, twid_sin)]
    return low + wide + [features]


def sin_cos(x):
    turns = jnp.floor(x * (1.0 / math.pi) + 0.5)
    rest = x - turns * 3.140625
    rest = rest - turns * 9.67502593994140625e-4
    rest = rest - turns * 1.509957990978376432e-7
    sign = 1.0 - 2.0 * (turns - 2.0 * jnp.floor(turns * 0.5))
    square = rest * rest
    odd = 1.0 / 6227020800.0
    for term in (-1.0 / 39916800.0, 1.0 / 362880.0, -1.0 / 5040.0, 1.0 / 120.0, -1.0 / 6.0, 1.0):
        odd = odd * square + term
    even = 1.0 / 479001600.0
    for term in (-1.0 / 3628800.0, 1.0 / 40320.0, -1.0 / 720.0, 1.0 / 24.0, -0.5, 1.0):
        even = even * square + term
    return sign * rest * odd, sign * even


def short_dot(left, right):
    return jnp.dot(left, right, preferred_element_type=jnp.float32)


def contract_dims(left, right, left_dim, right_dim):
    return lax.dot_general(
        left, right, (((left_dim,), (right_dim,)), ((), ())), preferred_element_type=jnp.float32
    )


def halves(x):
    upper = x.astype(jnp.bfloat16)
    return upper, (x - upper.astype(jnp.float32)).astype(jnp.bfloat16)


def split_dot(left, right):
    return contract_dims(
        jnp.concatenate([left[0], left[1], left[0]], axis=0),
        jnp.concatenate([right[0], right[0], right[1]], axis=0),
        0,
        0,
    )


def as_column(row, count):
    width = row.shape[1]
    diagonal = lax.broadcasted_iota(jnp.int32, (count, width), 0) == lax.broadcasted_iota(
        jnp.int32, (count, width), 1
    )
    return jnp.sum(jnp.where(diagonal, row, 0.0), axis=1, keepdims=True)


def operator_kernel(
    devices,
    channels,
    features_used,
    value_ref,
    first_ref,
    second_ref,
    cot_ref,
    pos_weight_hbm,
    pos_bias_hbm,
    mid_weight_hbm,
    mid_bias_hbm,
    out_weight_hbm,
    rates_hbm,
    left_fwd_hbm,
    left_inv_hbm,
    right_fwd_hbm,
    right_inv_hbm,
    twid_cos_hbm,
    twid_sin_hbm,
    features_hbm,
    value_out,
    first_out,
    second_out,
    out_weight_out,
    small_out,
    recv,
    outs,
    small_part,
    small_recv,
    small_sum,
    in_send,
    in_recv,
    out_send,
    out_recv,
    part_send,
    part_recv,
    sum_send,
    sum_recv,
    pos_weight_ref,
    pos_bias_ref,
    mid_weight_ref,
    mid_bias_ref,
    out_weight_ref,
    rates_ref,
    left_fwd_ref,
    left_inv_ref,
    right_fwd_ref,
    right_inv_ref,
    twid_cos_ref,
    twid_sin_ref,
    features_ref,
    pos_table,
    load_sem,
    own_sem,
):
    n = devices
    me = lax.axis_index("seq")
    width = RADIX
    seq_len = n * width
    groups = channels // GROUP
    rows_half = 2 * n * GROUP
    half_rows = n * GROUP
    bf16 = jnp.bfloat16
    f32 = jnp.float32

    barrier = pltpu.get_barrier_semaphore()

    def greet(step, carry):
        pl.semaphore_signal(
            barrier, inc=1, device_id={"seq": lax.rem(me + step, n)}, device_id_type=MESH
        )
        return carry

    lax.fori_loop(1, n, greet, 0)

    inputs = (value_ref, first_ref, cot_ref, second_ref)
    own_rows = pl.ds(pl.multiple_of(me * channels, channels), channels)
    pair = lax.rem(me, 2)
    column = me // 2
    loads = [
        pltpu.make_async_copy(source, target, load_sem.at[at])
        for at, (source, target) in enumerate(
            (
                (pos_weight_hbm, pos_weight_ref),
                (pos_bias_hbm, pos_bias_ref),
                (features_hbm, features_ref),
                (mid_weight_hbm, mid_weight_ref),
                (mid_bias_hbm, mid_bias_ref),
                (out_weight_hbm.at[:, pl.ds(pl.multiple_of(column * 128, 128), 128)], out_weight_ref),
                (rates_hbm, rates_ref),
                (left_fwd_hbm, left_fwd_ref),
                (right_fwd_hbm, right_fwd_ref),
                (twid_cos_hbm, twid_cos_ref),
                (twid_sin_hbm, twid_sin_ref),
                (right_inv_hbm, right_inv_ref),
                (left_inv_hbm, left_inv_ref),
            )
        )
    ]
    for load in loads:
        load.start()
    own_loads = [
        pltpu.make_async_copy(inputs[at].at[own_rows, :], recv.at[at, me], own_sem.at[at])
        for at in range(4)
    ]
    for load in own_loads:
        load.start()
    pl.semaphore_wait(barrier, n - 1)

    outputs = (second_out, first_out, value_out)

    def in_copy(at, peer, slot):
        return pltpu.make_async_remote_copy(
            src_ref=inputs[at].at[pl.ds(pl.multiple_of(peer * channels, channels), channels), :],
            dst_ref=recv.at[at, slot],
            send_sem=in_send.at[at, peer],
            recv_sem=in_recv.at[at, slot],
            device_id={"seq": peer},
            device_id_type=MESH,
        )

    def out_copy(at, peer, slot):
        return pltpu.make_async_remote_copy(
            src_ref=outs.at[at, peer],
            dst_ref=outputs[at].at[pl.ds(pl.multiple_of(slot * channels, channels), channels), :],
            send_sem=out_send.at[at, peer],
            recv_sem=out_recv.at[at, slot],
            device_id={"seq": peer},
            device_id_type=MESH,
        )

    def part_copy(peer, slot):
        return pltpu.make_async_remote_copy(
            src_ref=small_part.at[peer],
            dst_ref=small_recv.at[slot],
            send_sem=part_send.at[peer],
            recv_sem=part_recv.at[slot],
            device_id={"seq": peer},
            device_id_type=MESH,
        )

    def sum_copy(peer, slot):
        return pltpu.make_async_remote_copy(
            src_ref=small_sum,
            dst_ref=small_out.at[slot],
            send_sem=sum_send.at[peer],
            recv_sem=sum_recv.at[slot],
            device_id={"seq": peer},
            device_id_type=MESH,
        )

    def for_peers(action):
        def body(step, carry):
            action(lax.rem(me + step, n))
            return carry

        lax.fori_loop(1, n, body, 0)

    for at in range(2):
        for_peers(lambda peer, at=at: in_copy(at, peer, me).start())

    pos_table[...] = jnp.zeros_like(pos_table)
    for load in loads[:7]:
        load.wait()
    pos_table[0:features_used, :] = pos_weight_ref[...]
    pos_table[features_used : features_used + 1, :] = pos_bias_ref[...]
    features = features_ref[0:64, :]
    pre_one = split_dot(halves(pos_table[...]), (features, features_ref[64:128, :]))
    act_one, slope_one = sin_cos(pre_one)
    act_one = halves(act_one)
    mid_weight = mid_weight_ref[...]
    pre_two = split_dot(halves(mid_weight.T), act_one) + as_column(mid_bias_ref[...], 64)
    act_two, slope_two = sin_cos(pre_two)
    act_two = halves(act_two)

    def wanted(row):
        return jnp.where(row < channels, 2 * row, 2 * (row - channels) + 1) + 2 * channels * pair

    lane = lax.broadcasted_iota(jnp.int32, (2 * channels, 128), 1)
    row = lax.broadcasted_iota(jnp.int32, (2 * channels, 128), 0)
    rates_row = rates_ref[pl.ds(column, 1), :]
    own_rates = jnp.sum(jnp.where(lane == wanted(row), rates_row, 0.0), axis=1, keepdims=True)
    pick = lax.broadcasted_iota(jnp.int32, (128, 2 * channels), 0) == wanted(
        lax.broadcasted_iota(jnp.int32, (128, 2 * channels), 1)
    )
    pick = jnp.where(pick, 1.0, 0.0).astype(bf16)
    own_weight = tuple(
        short_dot(half, pick).astype(bf16) for half in halves(out_weight_ref[...])
    )
    ramp = lax.broadcasted_iota(jnp.int32, (1, seq_len), 1).astype(f32) * (1.0 / seq_len)
    window = jnp.exp(-own_rates * ramp)
    filters = (split_dot(own_weight, act_two) * window).astype(bf16)
    for at in range(2, 4):
        for_peers(lambda peer, at=at: in_copy(at, peer, me).start())
    for load in loads[7:]:
        load.wait()

    def to_sections(rows):
        return jnp.concatenate(
            [
                jnp.concatenate(
                    [
                        rows[GROUP * g : GROUP * (g + 1), width * at : width * (at + 1)]
                        for at in range(n)
                    ],
                    axis=0,
                )
                for g in range(groups)
            ],
            axis=1,
        )

    def from_sections(data):
        return jnp.concatenate(
            [
                jnp.concatenate(
                    [
                        data[GROUP * at : GROUP * (at + 1), width * g : width * (g + 1)]
                        for at in range(n)
                    ],
                    axis=1,
                )
                for g in range(groups)
            ],
            axis=0,
        )

    def forward(data):
        stage = short_dot(left_fwd_ref[...], data)
        cos, sin = twid_cos_ref[...], twid_sin_ref[...]
        result = []
        for g in range(groups):
            real = stage[:rows_half, width * g : width * (g + 1)]
            imag = stage[rows_half:, width * g : width * (g + 1)]
            real_b = (real * cos + imag * sin).astype(bf16)
            imag_b = (imag * cos - real * sin).astype(bf16)
            spectrum = short_dot(jnp.concatenate([real_b, imag_b], axis=1), right_fwd_ref[...])
            result.append((spectrum[:, :width], spectrum[:, width:]))
        return result

    def inverse(left, right, conj_left, conj_right):
        cos, sin = twid_cos_ref[...], twid_sin_ref[...]
        sections = []
        for g in range(groups):
            real_p, imag_p = spectral_product(left[g], right[g], conj_left, conj_right)
            stage = short_dot(jnp.concatenate([real_p, imag_p], axis=1), right_inv_ref[...])
            real, imag = stage[:, :width], stage[:, width:]
            real_r = (real * cos - imag * sin).astype(bf16)
            imag_r = (imag * cos + real * sin).astype(bf16)
            sections.append(jnp.concatenate([real_r, imag_r], axis=0))
        return short_dot(left_inv_ref[...], jnp.concatenate(sections, axis=1))

    def arrived(at):
        own_loads[at].wait()
        for_peers(lambda peer: in_copy(at, peer, peer).wait_recv())
        return jnp.concatenate(
            [
                recv[at, :, GROUP * g : GROUP * (g + 1), :].reshape(half_rows, width)
                for g in range(groups)
            ],
            axis=1,
        )

    def send_out(at, data):
        for g in range(groups):
            outs[at, :, GROUP * g : GROUP * (g + 1), :] = data[
                :, width * g : width * (g + 1)
            ].reshape(n, GROUP, width)
        for_peers(lambda peer: out_copy(at, peer, me).start())
        outputs[at][own_rows, :] = outs[at, me]

    spec_one = forward(to_sections(filters[:channels]))
    spec_two = forward(to_sections(filters[channels:]))
    spec_val = forward(arrived(0))
    conv_one = inverse(spec_one, spec_val, False, False)
    first = arrived(1).astype(f32)
    spec_gated = forward((first * conv_one).astype(bf16))
    conv_two = inverse(spec_two, spec_gated, False, False)
    cot = arrived(2).astype(f32)
    send_out(0, (cot * conv_two).astype(bf16))
    second = arrived(3).astype(f32)
    spec_gtwo = forward((cot * second).astype(bf16))
    gated_grad = inverse(spec_two, spec_gtwo, True, False)
    send_out(1, (gated_grad * conv_one).astype(bf16))
    spec_gone = forward((gated_grad * first).astype(bf16))
    send_out(2, inverse(spec_one, spec_gone, True, False).astype(bf16))
    filt_one = from_sections(inverse(spec_gone, spec_val, False, True))
    filt_two = from_sections(inverse(spec_gtwo, spec_gated, False, True))
    filter_grad = jnp.concatenate([filt_one, filt_two], axis=0) * window * (1.0 / seq_len)

    filter_grad = filter_grad.astype(bf16)
    pre_two_grad = (short_dot(own_weight[0], filter_grad) * slope_two).astype(bf16)
    pre_one_grad = contract_dims(mid_weight.astype(bf16), pre_two_grad, 0, 0) * slope_one
    both = contract_dims(
        jnp.concatenate([pre_two_grad, pre_one_grad.astype(bf16)], axis=0),
        jnp.concatenate([act_one[0], features], axis=0),
        1,
        1,
    )
    lane = lax.broadcasted_iota(jnp.int32, (64, 128), 1)
    from_two = (lane < 64) | (lane == 64 + features_used + 1)
    small = jnp.where(from_two, both[:64], both[64:])
    share = small.shape[0] // n
    for at in range(n):
        small_part[at] = small[share * at : share * (at + 1), :]
    for_peers(lambda peer: part_copy(peer, me).start())
    small_recv[me] = small_part[me]

    weight_grad = contract_dims(filter_grad, act_two[0], 1, 1)
    for o in range(2):
        out_weight_out[pl.ds(o, channels, stride=2), :] = weight_grad[
            channels * o : channels * (o + 1)
        ]

    for at in range(4):
        for_peers(lambda peer, at=at: in_copy(at, peer, me).wait_send())
    for at in range(2):
        for_peers(lambda peer, at=at: out_copy(at, peer, me).wait_send())
        for_peers(lambda peer, at=at: out_copy(at, peer, peer).wait_recv())
    for_peers(lambda peer: part_copy(peer, peer).wait_recv())
    total = small_recv[0]
    for at in range(1, n):
        total = total + small_recv[at]
    small_sum[...] = total
    small_out[me] = total
    for_peers(lambda peer: sum_copy(peer, me).start())

    for_peers(lambda peer: out_copy(2, peer, me).wait_send())
    for_peers(lambda peer: out_copy(2, peer, peer).wait_recv())
    for_peers(lambda peer: part_copy(peer, me).wait_send())
    for_peers(lambda peer: sum_copy(peer, me).wait_send())
    for_peers(lambda peer: sum_copy(peer, peer).wait_recv())


def finish_kernel(
    features_used,
    value_in,
    first_in,
    second_in,
    weight_in,
    small_in,
    value_out,
    first_out,
    second_out,
    weight_out,
    pos_weight_out,
    pos_bias_out,
    mid_weight_out,
    mid_bias_out,
    value_ref,
    first_ref,
    second_ref,
    weight_ref,
    small_ref,
    in_sem,
    out_sem,
):
    sources = (small_in, value_in, first_in, second_in, weight_in)
    held = (small_ref, value_ref, first_ref, second_ref, weight_ref)
    targets = (None, value_out, first_out, second_out, weight_out)
    loads = [
        pltpu.make_async_copy(sources[at], held[at], in_sem.at[at]) for at in range(5)
    ]
    stores = [
        pltpu.make_async_copy(held[at], targets[at], out_sem.at[at]) for at in range(1, 5)
    ]
    for load in loads:
        load.start()
    for load, store in zip(loads[1:], stores):
        load.wait()
        store.start()
    loads[0].wait()
    small = small_ref[...]
    turned = small.T
    last = 64 + features_used
    pos_weight_out[...] = turned[64:last]
    pos_bias_out[...] = turned[last : last + 1]
    mid_bias_out[...] = turned[last + 1 : last + 2]
    mid_weight_out[...] = small[:, :64]
    for store in stores:
        store.wait()


def on_device(
    value_branch,
    first_gate,
    second_gate,
    out_cotangent,
    pos_weight,
    pos_bias,
    mid_weight,
    mid_bias,
    out_weight,
    decay_rates,
):
    model_width, tok_dev = value_branch.shape
    devices = lax.axis_size("seq")
    channels = model_width // devices
    hidden, features_used = pos_weight.shape
    fits = (
        tok_dev == RADIX
        and devices == 16
        and channels == 2 * GROUP
        and hidden == 64
        and features_used <= 61
        and out_weight.shape == (2 * model_width, 64)
    )
    if not fits:
        return on_device_plain(
            value_branch,
            first_gate,
            second_gate,
            out_cotangent,
            pos_weight,
            pos_bias,
            mid_weight,
            mid_bias,
            out_weight,
            decay_rates,
        )
    seq_len = tok_dev * devices
    freq_rows = 2 * devices
    tables = numpy_tables(freq_rows, RADIX, seq_len, (features_used - 1) // 2, GROUP)
    share = hidden // devices
    dma = pltpu.SemaphoreType.DMA
    vmem = pl.BlockSpec(memory_space=pltpu.VMEM)
    hbm = pl.BlockSpec(memory_space=pltpu.HBM)
    bf16, f32 = jnp.bfloat16, jnp.float32
    value_out, first_out, second_out, weight_out, small = pl.pallas_call(
        functools.partial(operator_kernel, devices, channels, features_used),
        out_shape=[jax.ShapeDtypeStruct((model_width, tok_dev), jnp.bfloat16)] * 3
        + [
            jax.ShapeDtypeStruct((2 * channels, hidden), jnp.float32),
            jax.ShapeDtypeStruct((devices, share, 2 * hidden), jnp.float32),
        ],
        in_specs=[hbm] * 17,
        out_specs=[vmem] * 5,
        scratch_shapes=[
            pltpu.VMEM((4, devices, channels, RADIX), jnp.bfloat16),
            pltpu.VMEM((3, devices, channels, RADIX), jnp.bfloat16),
            pltpu.VMEM((devices, share, 2 * hidden), jnp.float32),
            pltpu.VMEM((devices, share, 2 * hidden), jnp.float32),
            pltpu.VMEM((share, 2 * hidden), jnp.float32),
            dma((4, devices)),
            dma((4, devices)),
            dma((3, devices)),
            dma((3, devices)),
            dma((devices,)),
            dma((devices,)),
            dma((devices,)),
            dma((devices,)),
            pltpu.VMEM((features_used, hidden), f32),
            pltpu.VMEM((1, hidden), f32),
            pltpu.VMEM((hidden, hidden), f32),
            pltpu.VMEM((1, hidden), f32),
            pltpu.VMEM((hidden, 128), f32),
            pltpu.VMEM((2 * model_width // 128, 128), f32),
            *[pltpu.VMEM(table.shape, table.dtype) for table in tables],
            pltpu.VMEM((hidden, hidden), f32),
            dma((13,)),
            dma((4,)),
        ],
        compiler_params=pltpu.CompilerParams(
            collective_id=0, has_side_effects=True, vmem_limit_bytes=62 * 1024 * 1024
        ),
    )(
        value_branch,
        first_gate,
        second_gate,
        out_cotangent,
        pos_weight.T,
        pos_bias.reshape(1, hidden),
        mid_weight,
        mid_bias.reshape(1, hidden),
        out_weight.T,
        decay_rates.reshape(2 * model_width // 128, 128),
        *[jnp.asarray(table) for table in tables],
    )
    small = small.reshape(hidden, 2 * hidden)
    shape = jax.ShapeDtypeStruct
    results = pl.pallas_call(
        functools.partial(finish_kernel, features_used),
        out_shape=[shape((model_width, tok_dev), bf16)] * 3
        + [
            shape((2 * channels, hidden), f32),
            shape((features_used, hidden), f32),
            shape((1, hidden), f32),
            shape((hidden, hidden), f32),
            shape((1, hidden), f32),
        ],
        in_specs=[hbm] * 5,
        out_specs=[hbm] * 4 + [pl.BlockSpec()] * 4,
        scratch_shapes=[pltpu.VMEM((model_width, tok_dev), bf16)] * 3
        + [
            pltpu.VMEM((2 * channels, hidden), f32),
            pltpu.VMEM((hidden, 2 * hidden), f32),
            dma((5,)),
            dma((5,)),
        ],
        compiler_params=pltpu.CompilerParams(vmem_limit_bytes=62 * 1024 * 1024),
    )(value_out, first_out, second_out, weight_out, small)
    return (
        results[0],
        results[1],
        results[2],
        results[4].T,
        results[5].reshape(hidden),
        results[6],
        results[7].reshape(hidden),
        results[3],
    )


def solution(mesh):
    in_specs = (
        P(None, ("dp", "seq")),
        P(None, ("dp", "seq")),
        P(None, ("dp", "seq")),
        P(None, ("dp", "seq")),
        P(),
        P(),
        P(),
        P(),
        P(),
        P(),
    )
    out_specs = (
        P(None, ("dp", "seq")),
        P(None, ("dp", "seq")),
        P(None, ("dp", "seq")),
        P("dp", None),
        P("dp"),
        P("dp", None),
        P("dp"),
        P("seq", "dp"),
    )
    return jax.shard_map(
        on_device, mesh=mesh, in_specs=in_specs, out_specs=out_specs, check_vma=False
    )
```

```python
import functools
import math

import jax
import jax.numpy as jnp
import ml_dtypes
import numpy as np
from jax import lax
from jax.experimental import pallas as pl
from jax.experimental.pallas import tpu as pltpu
from jax.sharding import PartitionSpec as P

RADIX = 128
GROUP = 16
MESH = pl.DeviceIdType.MESH


def make_tables(freq_rows, radix):
    length_all = freq_rows * radix
    freq_index = jnp.arange(freq_rows, dtype=jnp.int32)
    half_index = jnp.arange(freq_rows // 2, dtype=jnp.int32)
    inner_index = jnp.arange(radix, dtype=jnp.int32)
    angle_one = (freq_index[:, None] * half_index[None, :] % freq_rows).astype(jnp.float32) * (
        2.0 * math.pi / freq_rows
    )
    angle_two = (inner_index[:, None] * inner_index[None, :] % radix).astype(jnp.float32) * (
        2.0 * math.pi / radix
    )
    angle_twid = (freq_index[:, None] * inner_index[None, :] % length_all).astype(jnp.float32) * (
        2.0 * math.pi / length_all
    )
    cos_one = jnp.cos(angle_one).astype(jnp.bfloat16)
    sin_one = jnp.sin(angle_one).astype(jnp.bfloat16)
    cos_two = jnp.cos(angle_two).astype(jnp.bfloat16)
    sin_two = jnp.sin(angle_two).astype(jnp.bfloat16)
    left_table = jnp.concatenate([cos_one, -sin_one], axis=0)
    right_fwd = jnp.concatenate(
        [jnp.concatenate([cos_two, -sin_two], axis=1), jnp.concatenate([sin_two, cos_two], axis=1)],
        axis=0,
    )
    right_inv = jnp.concatenate(
        [jnp.concatenate([cos_two, sin_two], axis=1), jnp.concatenate([-sin_two, cos_two], axis=1)],
        axis=0,
    )
    return (left_table, right_fwd, right_inv, jnp.cos(angle_twid), jnp.sin(angle_twid))


def forward_spectrum(signal, tables, freq_rows, radix):
    left_table, right_fwd, right_inv, twid_cos, twid_sin = tables
    count = signal.shape[0]
    shaped = signal.reshape(count, freq_rows // 2, radix)
    stacked = jnp.einsum("kn,rnm->rkm", left_table, shaped, preferred_element_type=jnp.float32)
    real_a = stacked[:, :freq_rows]
    imag_a = stacked[:, freq_rows:]
    real_b = (real_a * twid_cos + imag_a * twid_sin).astype(jnp.bfloat16)
    imag_b = (imag_a * twid_cos - real_a * twid_sin).astype(jnp.bfloat16)
    joined = jnp.concatenate([real_b, imag_b], axis=2)
    spectrum = jnp.einsum("rkn,nm->rkm", joined, right_fwd, preferred_element_type=jnp.float32)
    return (spectrum[:, :, :radix], spectrum[:, :, radix:])


def inverse_signal(product, tables, freq_rows, radix):
    left_table, right_fwd, right_inv, twid_cos, twid_sin = tables
    real_p, imag_p = product
    joined = jnp.concatenate([real_p, imag_p], axis=2)
    section_q = jnp.einsum("rkn,nm->rkm", joined, right_inv, preferred_element_type=jnp.float32)
    real_q = section_q[:, :, :radix]
    imag_q = section_q[:, :, radix:]
    real_r = (real_q * twid_cos - imag_q * twid_sin).astype(jnp.bfloat16)
    imag_r = (imag_q * twid_cos + real_q * twid_sin).astype(jnp.bfloat16)
    rows_both = jnp.concatenate([real_r, imag_r], axis=1)
    output = jnp.einsum("kn,rkm->rnm", left_table, rows_both, preferred_element_type=jnp.float32)
    count = real_p.shape[0]
    return (output * (1.0 / (freq_rows * radix))).reshape(count, freq_rows // 2 * radix)


def spectral_product(left, right, conj_left, conj_right):
    sign_left = -1.0 if conj_left else 1.0
    sign_right = -1.0 if conj_right else 1.0
    real_part = left[0] * right[0] - sign_left * sign_right * left[1] * right[1]
    imag_part = sign_left * left[1] * right[0] + sign_right * left[0] * right[1]
    return (real_part.astype(jnp.bfloat16), imag_part.astype(jnp.bfloat16))


def positional_features(positions, seq_len, bands):
    band_index = jnp.arange(1, bands + 1, dtype=jnp.int32)
    angles = (band_index[:, None] * positions[None, :] % seq_len).astype(jnp.float32) * (
        2.0 * math.pi / seq_len
    )
    ramp = positions.astype(jnp.float32)[None, :] / seq_len
    return jnp.concatenate([ramp, jnp.cos(angles), jnp.sin(angles)], axis=0)


def filter_network(positions, seq_len, pos_weight, pos_bias, mid_weight, mid_bias):
    bands = (pos_weight.shape[1] - 1) // 2
    features = positional_features(positions, seq_len, bands)
    pre_one = jnp.dot(pos_weight, features, precision=lax.Precision.HIGHEST) + pos_bias[:, None]
    act_one = jnp.sin(pre_one)
    pre_two = jnp.dot(mid_weight, act_one, precision=lax.Precision.HIGHEST) + mid_bias[:, None]
    act_two = jnp.sin(pre_two)
    return (features, pre_one, act_one, pre_two, act_two)


def modulation(rates, positions, seq_len):
    return jnp.exp(-rates[:, None] * positions.astype(jnp.float32)[None, :] / seq_len)


def contract_last(left, right):
    return lax.dot_general(left, right, (((1,), (1,)), ((), ())), precision=lax.Precision.HIGHEST)


def network_backward(act_grad, features, pre_one, act_one, pre_two, mid_weight):
    pre_two_grad = act_grad * jnp.cos(pre_two)
    mid_weight_part = contract_last(pre_two_grad, act_one)
    mid_bias_part = jnp.sum(pre_two_grad, axis=1)
    pre_one_grad = jnp.dot(mid_weight.T, pre_two_grad, precision=lax.Precision.HIGHEST) * jnp.cos(
        pre_one
    )
    pos_weight_part = contract_last(pre_one_grad, features)
    pos_bias_part = jnp.sum(pre_one_grad, axis=1)
    return (pos_weight_part, pos_bias_part, mid_weight_part, mid_bias_part)


def on_device_plain(
    value_branch,
    first_gate,
    second_gate,
    out_cotangent,
    pos_weight,
    pos_bias,
    mid_weight,
    mid_bias,
    out_weight,
    decay_rates,
):
    model_width, tok_dev = value_branch.shape
    devices = lax.axis_size("seq")
    seq_len = tok_dev * devices
    channels = model_width // devices
    my_rank = lax.axis_index("seq")
    freq_rows = 2 * seq_len // RADIX
    tables = make_tables(freq_rows, RADIX)
    all_positions = jnp.arange(seq_len, dtype=jnp.int32)
    own_rates = lax.dynamic_slice_in_dim(decay_rates, my_rank * 2 * channels, 2 * channels)
    window_own = modulation(own_rates, all_positions, seq_len)
    value_ch, first_ch = (
        lax.all_to_all(value_branch, "seq", split_axis=0, concat_axis=1, tiled=True),
        lax.all_to_all(first_gate, "seq", split_axis=0, concat_axis=1, tiled=True),
    )
    local_positions = my_rank * tok_dev + jnp.arange(tok_dev, dtype=jnp.int32)
    features, pre_one, act_one, pre_two, act_two = filter_network(
        local_positions, seq_len, pos_weight, pos_bias, mid_weight, mid_bias
    )
    window_local = modulation(decay_rates, local_positions, seq_len)
    local_filters = (
        jnp.dot(out_weight, act_two, precision=lax.Precision.HIGHEST) * window_local
    ).astype(jnp.bfloat16)
    filt_ch = lax.all_to_all(local_filters, "seq", split_axis=0, concat_axis=1, tiled=True)
    filt_real, filt_imag = forward_spectrum(filt_ch, tables, freq_rows, RADIX)
    filt_real = filt_real.reshape(channels, 2, freq_rows, RADIX)
    filt_imag = filt_imag.reshape(channels, 2, freq_rows, RADIX)
    spec_one = (filt_real[:, 0], filt_imag[:, 0])
    spec_two = (filt_real[:, 1], filt_imag[:, 1])
    spec_val = forward_spectrum(value_ch, tables, freq_rows, RADIX)
    conv_one = inverse_signal(
        spectral_product(spec_one, spec_val, False, False), tables, freq_rows, RADIX
    )
    gated = (first_ch.astype(jnp.float32) * conv_one).astype(jnp.bfloat16)
    spec_gated = forward_spectrum(gated, tables, freq_rows, RADIX)
    conv_two = inverse_signal(
        spectral_product(spec_two, spec_gated, False, False), tables, freq_rows, RADIX
    )
    second_ch, cot_ch = (
        lax.all_to_all(second_gate, "seq", split_axis=0, concat_axis=1, tiled=True),
        lax.all_to_all(out_cotangent, "seq", split_axis=0, concat_axis=1, tiled=True),
    )
    cot_wide = cot_ch.astype(jnp.float32)
    second_grad_ch = (cot_wide * conv_two).astype(jnp.bfloat16)
    second_out = lax.all_to_all(second_grad_ch, "seq", split_axis=1, concat_axis=0, tiled=True)
    grad_two = (cot_wide * second_ch.astype(jnp.float32)).astype(jnp.bfloat16)
    spec_gtwo = forward_spectrum(grad_two, tables, freq_rows, RADIX)
    gated_grad = inverse_signal(
        spectral_product(spec_two, spec_gtwo, True, False), tables, freq_rows, RADIX
    )
    filt_grad_two = inverse_signal(
        spectral_product(spec_gtwo, spec_gated, False, True), tables, freq_rows, RADIX
    )
    first_grad_ch = (gated_grad * conv_one).astype(jnp.bfloat16)
    grad_one = (gated_grad * first_ch.astype(jnp.float32)).astype(jnp.bfloat16)
    spec_gone = forward_spectrum(grad_one, tables, freq_rows, RADIX)
    value_grad_ch = inverse_signal(
        spectral_product(spec_one, spec_gone, True, False), tables, freq_rows, RADIX
    ).astype(jnp.bfloat16)
    filt_grad_one = inverse_signal(
        spectral_product(spec_gone, spec_val, False, True), tables, freq_rows, RADIX
    )
    value_out, first_out = (
        lax.all_to_all(value_grad_ch, "seq", split_axis=1, concat_axis=0, tiled=True),
        lax.all_to_all(first_grad_ch, "seq", split_axis=1, concat_axis=0, tiled=True),
    )
    filt_grads = jnp.stack([filt_grad_one, filt_grad_two], axis=1).reshape(2 * channels, seq_len)
    filter_grad_ch = filt_grads * window_own / seq_len
    filter_grad_seq = lax.all_to_all(
        filter_grad_ch.astype(jnp.bfloat16), "seq", split_axis=1, concat_axis=0, tiled=True
    ).astype(filter_grad_ch.dtype)
    out_weight_grad = lax.psum_scatter(
        contract_last(filter_grad_seq, act_two), "seq", scatter_dimension=0, tiled=True
    )
    act_grad = jnp.dot(out_weight.T, filter_grad_seq, precision=lax.Precision.HIGHEST)
    partials = network_backward(act_grad, features, pre_one, act_one, pre_two, mid_weight)
    pos_weight_grad, pos_bias_grad, mid_weight_grad, mid_bias_grad = lax.psum(
        (partials[0], partials[1], partials[2], partials[3]), "seq"
    )
    return (
        value_out,
        first_out,
        second_out,
        pos_weight_grad,
        pos_bias_grad,
        mid_weight_grad,
        mid_bias_grad,
        out_weight_grad,
    )


def numpy_tables(freq_rows, radix, seq_len, bands, group):
    half = freq_rows // 2
    length_all = freq_rows * radix
    freq_index = np.arange(freq_rows)
    inner = np.arange(radix)
    angle_one = (freq_index[:, None] * np.arange(half)[None, :] % freq_rows) * (2.0 * np.pi / freq_rows)
    angle_two = (inner[:, None] * inner[None, :] % radix) * (2.0 * np.pi / radix)
    angle_twid = (freq_index[:, None] * inner[None, :] % length_all) * (2.0 * np.pi / length_all)
    left = np.concatenate([np.cos(angle_one), -np.sin(angle_one)], axis=0)
    left_fwd = np.kron(left, np.eye(group))
    left_inv = left_fwd.T / length_all
    cos_two, sin_two = np.cos(angle_two), np.sin(angle_two)
    right_fwd = np.block([[cos_two, -sin_two], [sin_two, cos_two]])
    right_inv = np.block([[cos_two, sin_two], [-sin_two, cos_two]])
    twid_cos = np.repeat(np.cos(angle_twid), group, axis=0)
    twid_sin = np.repeat(np.sin(angle_twid), group, axis=0)
    positions = np.arange(seq_len)
    band = np.arange(1, bands + 1)
    angles = (band[:, None] * positions[None, :] % seq_len) * (2.0 * np.pi / seq_len)
    features = np.zeros((64, seq_len), np.float32)
    features[0] = positions / seq_len
    features[1 : bands + 1] = np.cos(angles)
    features[bands + 1 : 2 * bands + 1] = np.sin(angles)
    features[2 * bands + 1 : 2 * bands + 3] = 1.0
    upper = features.astype(ml_dtypes.bfloat16)
    lower = (features - upper.astype(np.float32)).astype(ml_dtypes.bfloat16)
    features = np.concatenate([upper, lower], axis=0)
    low = [table.astype(ml_dtypes.bfloat16) for table in (left_fwd, left_inv, right_fwd, right_inv)]
    wide = [table.astype(np.float32) for table in (twid_cos, twid_sin)]
    return low + wide + [features]


def sin_cos(x):
    turns = jnp.floor(x * (1.0 / math.pi) + 0.5)
    rest = x - turns * 3.140625
    rest = rest - turns * 9.67502593994140625e-4
    rest = rest - turns * 1.509957990978376432e-7
    sign = 1.0 - 2.0 * (turns - 2.0 * jnp.floor(turns * 0.5))
    square = rest * rest
    odd = 1.0 / 6227020800.0
    for term in (-1.0 / 39916800.0, 1.0 / 362880.0, -1.0 / 5040.0, 1.0 / 120.0, -1.0 / 6.0, 1.0):
        odd = odd * square + term
    even = 1.0 / 479001600.0
    for term in (-1.0 / 3628800.0, 1.0 / 40320.0, -1.0 / 720.0, 1.0 / 24.0, -0.5, 1.0):
        even = even * square + term
    return sign * rest * odd, sign * even


def short_dot(left, right):
    return jnp.dot(left, right, preferred_element_type=jnp.float32)


def contract_dims(left, right, left_dim, right_dim):
    return lax.dot_general(
        left, right, (((left_dim,), (right_dim,)), ((), ())), preferred_element_type=jnp.float32
    )


def halves(x):
    upper = x.astype(jnp.bfloat16)
    return upper, (x - upper.astype(jnp.float32)).astype(jnp.bfloat16)


def split_dot(left, right):
    return contract_dims(
        jnp.concatenate([left[0], left[1], left[0]], axis=0),
        jnp.concatenate([right[0], right[0], right[1]], axis=0),
        0,
        0,
    )


def as_column(row, count):
    width = row.shape[1]
    diagonal = lax.broadcasted_iota(jnp.int32, (count, width), 0) == lax.broadcasted_iota(
        jnp.int32, (count, width), 1
    )
    return jnp.sum(jnp.where(diagonal, row, 0.0), axis=1, keepdims=True)


def operator_kernel(
    devices,
    channels,
    features_used,
    value_ref,
    first_ref,
    second_ref,
    cot_ref,
    pos_weight_hbm,
    pos_bias_hbm,
    mid_weight_hbm,
    mid_bias_hbm,
    out_weight_hbm,
    rates_hbm,
    left_fwd_hbm,
    left_inv_hbm,
    right_fwd_hbm,
    right_inv_hbm,
    twid_cos_hbm,
    twid_sin_hbm,
    features_hbm,
    value_out,
    first_out,
    second_out,
    out_weight_out,
    small_out,
    recv,
    outs,
    small_part,
    small_recv,
    small_sum,
    in_send,
    in_recv,
    out_send,
    out_recv,
    part_send,
    part_recv,
    sum_send,
    sum_recv,
    pos_weight_ref,
    pos_bias_ref,
    mid_weight_ref,
    mid_bias_ref,
    out_weight_ref,
    rates_ref,
    left_fwd_ref,
    left_inv_ref,
    right_fwd_ref,
    right_inv_ref,
    twid_cos_ref,
    twid_sin_ref,
    features_ref,
    pos_table,
    load_sem,
    own_sem,
):
    n = devices
    me = lax.axis_index("seq")
    width = RADIX
    seq_len = n * width
    groups = channels // GROUP
    rows_half = 2 * n * GROUP
    half_rows = n * GROUP
    bf16 = jnp.bfloat16
    f32 = jnp.float32

    barrier = pltpu.get_barrier_semaphore()

    def greet(step, carry):
        pl.semaphore_signal(
            barrier, inc=1, device_id={"seq": lax.rem(me + step, n)}, device_id_type=MESH
        )
        return carry

    lax.fori_loop(1, n, greet, 0)

    inputs = (cot_ref, second_ref, first_ref, value_ref)
    own_rows = pl.ds(pl.multiple_of(me * channels, channels), channels)
    pair = lax.rem(me, 2)
    column = me // 2
    loads = [
        pltpu.make_async_copy(source, target, load_sem.at[at])
        for at, (source, target) in enumerate(
            (
                (pos_weight_hbm, pos_weight_ref),
                (pos_bias_hbm, pos_bias_ref),
                (features_hbm, features_ref),
                (mid_weight_hbm, mid_weight_ref),
                (mid_bias_hbm, mid_bias_ref),
                (out_weight_hbm.at[:, pl.ds(pl.multiple_of(column * 128, 128), 128)], out_weight_ref),
                (rates_hbm, rates_ref),
                (left_fwd_hbm, left_fwd_ref),
                (right_fwd_hbm, right_fwd_ref),
                (twid_cos_hbm, twid_cos_ref),
                (twid_sin_hbm, twid_sin_ref),
                (right_inv_hbm, right_inv_ref),
                (left_inv_hbm, left_inv_ref),
            )
        )
    ]
    for load in loads:
        load.start()
    own_loads = [
        pltpu.make_async_copy(inputs[at].at[own_rows, :], recv.at[at, me], own_sem.at[at])
        for at in range(4)
    ]
    for load in own_loads:
        load.start()
    pl.semaphore_wait(barrier, n - 1)

    outputs = (second_out, first_out, value_out)

    def in_copy(at, peer, slot):
        return pltpu.make_async_remote_copy(
            src_ref=inputs[at].at[pl.ds(pl.multiple_of(peer * channels, channels), channels), :],
            dst_ref=recv.at[at, slot],
            send_sem=in_send.at[at, peer],
            recv_sem=in_recv.at[at, slot],
            device_id={"seq": peer},
            device_id_type=MESH,
        )

    def out_copy(at, peer, slot):
        return pltpu.make_async_remote_copy(
            src_ref=outs.at[at, peer],
            dst_ref=outputs[at].at[pl.ds(pl.multiple_of(slot * channels, channels), channels), :],
            send_sem=out_send.at[at, peer],
            recv_sem=out_recv.at[at, slot],
            device_id={"seq": peer},
            device_id_type=MESH,
        )

    def part_copy(peer, slot):
        return pltpu.make_async_remote_copy(
            src_ref=small_part.at[peer],
            dst_ref=small_recv.at[slot],
            send_sem=part_send.at[peer],
            recv_sem=part_recv.at[slot],
            device_id={"seq": peer},
            device_id_type=MESH,
        )

    def sum_copy(peer, slot):
        return pltpu.make_async_remote_copy(
            src_ref=small_sum,
            dst_ref=small_out.at[slot],
            send_sem=sum_send.at[peer],
            recv_sem=sum_recv.at[slot],
            device_id={"seq": peer},
            device_id_type=MESH,
        )

    def for_peers(action):
        def body(step, carry):
            action(lax.rem(me + step, n))
            return carry

        lax.fori_loop(1, n, body, 0)

    for at in range(2):
        for_peers(lambda peer, at=at: in_copy(at, peer, me).start())

    pos_table[...] = jnp.zeros_like(pos_table)
    for load in loads[:7]:
        load.wait()
    pos_table[0:features_used, :] = pos_weight_ref[...]
    pos_table[features_used : features_used + 1, :] = pos_bias_ref[...]
    features = features_ref[0:64, :]
    pre_one = split_dot(halves(pos_table[...]), (features, features_ref[64:128, :]))
    act_one, slope_one = sin_cos(pre_one)
    act_one = halves(act_one)
    mid_weight = mid_weight_ref[...]
    pre_two = split_dot(halves(mid_weight.T), act_one) + as_column(mid_bias_ref[...], 64)
    act_two, slope_two = sin_cos(pre_two)
    act_two = halves(act_two)

    def wanted(row):
        return jnp.where(row < channels, 2 * row, 2 * (row - channels) + 1) + 2 * channels * pair

    lane = lax.broadcasted_iota(jnp.int32, (2 * channels, 128), 1)
    row = lax.broadcasted_iota(jnp.int32, (2 * channels, 128), 0)
    rates_row = rates_ref[pl.ds(column, 1), :]
    own_rates = jnp.sum(jnp.where(lane == wanted(row), rates_row, 0.0), axis=1, keepdims=True)
    pick = lax.broadcasted_iota(jnp.int32, (128, 2 * channels), 0) == wanted(
        lax.broadcasted_iota(jnp.int32, (128, 2 * channels), 1)
    )
    pick = jnp.where(pick, 1.0, 0.0).astype(bf16)
    own_weight = tuple(
        short_dot(half, pick).astype(bf16) for half in halves(out_weight_ref[...])
    )
    ramp = lax.broadcasted_iota(jnp.int32, (1, seq_len), 1).astype(f32) * (1.0 / seq_len)
    window = jnp.exp(-own_rates * ramp)
    filters = (split_dot(own_weight, act_two) * window).astype(bf16)
    for at in range(2, 4):
        for_peers(lambda peer, at=at: in_copy(at, peer, me).start())
    for load in loads[7:]:
        load.wait()

    def to_sections(rows):
        return jnp.concatenate(
            [
                jnp.concatenate(
                    [
                        rows[GROUP * g : GROUP * (g + 1), width * at : width * (at + 1)]
                        for at in range(n)
                    ],
                    axis=0,
                )
                for g in range(groups)
            ],
            axis=1,
        )

    def from_sections(data):
        return jnp.concatenate(
            [
                jnp.concatenate(
                    [
                        data[GROUP * at : GROUP * (at + 1), width * g : width * (g + 1)]
                        for at in range(n)
                    ],
                    axis=1,
                )
                for g in range(groups)
            ],
            axis=0,
        )

    def forward(data):
        stage = short_dot(left_fwd_ref[...], data)
        cos, sin = twid_cos_ref[...], twid_sin_ref[...]
        result = []
        for g in range(groups):
            real = stage[:rows_half, width * g : width * (g + 1)]
            imag = stage[rows_half:, width * g : width * (g + 1)]
            real_b = (real * cos + imag * sin).astype(bf16)
            imag_b = (imag * cos - real * sin).astype(bf16)
            spectrum = short_dot(jnp.concatenate([real_b, imag_b], axis=1), right_fwd_ref[...])
            result.append((spectrum[:, :width], spectrum[:, width:]))
        return result

    def inverse(left, right, conj_left, conj_right):
        cos, sin = twid_cos_ref[...], twid_sin_ref[...]
        sections = []
        for g in range(groups):
            real_p, imag_p = spectral_product(left[g], right[g], conj_left, conj_right)
            stage = short_dot(jnp.concatenate([real_p, imag_p], axis=1), right_inv_ref[...])
            real, imag = stage[:, :width], stage[:, width:]
            real_r = (real * cos - imag * sin).astype(bf16)
            imag_r = (imag * cos + real * sin).astype(bf16)
            sections.append(jnp.concatenate([real_r, imag_r], axis=0))
        return short_dot(left_inv_ref[...], jnp.concatenate(sections, axis=1))

    def arrived(at):
        own_loads[at].wait()
        for_peers(lambda peer: in_copy(at, peer, peer).wait_recv())
        return jnp.concatenate(
            [
                recv[at, :, GROUP * g : GROUP * (g + 1), :].reshape(half_rows, width)
                for g in range(groups)
            ],
            axis=1,
        )

    def send_out(at, data):
        for g in range(groups):
            outs[at, :, GROUP * g : GROUP * (g + 1), :] = data[
                :, width * g : width * (g + 1)
            ].reshape(n, GROUP, width)
        for_peers(lambda peer: out_copy(at, peer, me).start())
        outputs[at][own_rows, :] = outs[at, me]

    spec_one = forward(to_sections(filters[:channels]))
    spec_two = forward(to_sections(filters[channels:]))
    cot = arrived(0).astype(f32)
    second = arrived(1).astype(f32)
    spec_gtwo = forward((cot * second).astype(bf16))
    gated_grad = inverse(spec_two, spec_gtwo, True, False)
    first = arrived(2).astype(f32)
    spec_gone = forward((gated_grad * first).astype(bf16))
    send_out(2, inverse(spec_one, spec_gone, True, False).astype(bf16))
    spec_val = forward(arrived(3))
    conv_one = inverse(spec_one, spec_val, False, False)
    send_out(1, (gated_grad * conv_one).astype(bf16))
    spec_gated = forward((first * conv_one).astype(bf16))
    conv_two = inverse(spec_two, spec_gated, False, False)
    send_out(0, (cot * conv_two).astype(bf16))
    filt_one = from_sections(inverse(spec_gone, spec_val, False, True))
    filt_two = from_sections(inverse(spec_gtwo, spec_gated, False, True))
    filter_grad = jnp.concatenate([filt_one, filt_two], axis=0) * window * (1.0 / seq_len)

    filter_grad = filter_grad.astype(bf16)
    pre_two_grad = (short_dot(own_weight[0], filter_grad) * slope_two).astype(bf16)
    pre_one_grad = contract_dims(mid_weight.astype(bf16), pre_two_grad, 0, 0) * slope_one
    both = contract_dims(
        jnp.concatenate([pre_two_grad, pre_one_grad.astype(bf16)], axis=0),
        jnp.concatenate([act_one[0], features], axis=0),
        1,
        1,
    )
    lane = lax.broadcasted_iota(jnp.int32, (64, 128), 1)
    from_two = (lane < 64) | (lane == 64 + features_used + 1)
    small = jnp.where(from_two, both[:64], both[64:])
    share = small.shape[0] // n
    for at in range(n):
        small_part[at] = small[share * at : share * (at + 1), :]
    for_peers(lambda peer: part_copy(peer, me).start())
    small_recv[me] = small_part[me]

    weight_grad = contract_dims(filter_grad, act_two[0], 1, 1)
    for o in range(2):
        out_weight_out[pl.ds(o, channels, stride=2), :] = weight_grad[
            channels * o : channels * (o + 1)
        ]

    for at in range(4):
        for_peers(lambda peer, at=at: in_copy(at, peer, me).wait_send())
    for at in range(2):
        for_peers(lambda peer, at=at: out_copy(at, peer, me).wait_send())
        for_peers(lambda peer, at=at: out_copy(at, peer, peer).wait_recv())
    for_peers(lambda peer: part_copy(peer, peer).wait_recv())
    total = small_recv[0]
    for at in range(1, n):
        total = total + small_recv[at]
    small_sum[...] = total
    small_out[me] = total
    for_peers(lambda peer: sum_copy(peer, me).start())

    for_peers(lambda peer: out_copy(2, peer, me).wait_send())
    for_peers(lambda peer: out_copy(2, peer, peer).wait_recv())
    for_peers(lambda peer: part_copy(peer, me).wait_send())
    for_peers(lambda peer: sum_copy(peer, me).wait_send())
    for_peers(lambda peer: sum_copy(peer, peer).wait_recv())


def finish_kernel(
    features_used,
    value_in,
    first_in,
    second_in,
    weight_in,
    small_in,
    value_out,
    first_out,
    second_out,
    weight_out,
    pos_weight_out,
    pos_bias_out,
    mid_weight_out,
    mid_bias_out,
    value_ref,
    first_ref,
    second_ref,
    weight_ref,
    small_ref,
    in_sem,
    out_sem,
):
    sources = (small_in, value_in, first_in, second_in, weight_in)
    held = (small_ref, value_ref, first_ref, second_ref, weight_ref)
    targets = (None, value_out, first_out, second_out, weight_out)
    loads = [
        pltpu.make_async_copy(sources[at], held[at], in_sem.at[at]) for at in range(5)
    ]
    stores = [
        pltpu.make_async_copy(held[at], targets[at], out_sem.at[at]) for at in range(1, 5)
    ]
    for load in loads:
        load.start()
    for load, store in zip(loads[1:], stores):
        load.wait()
        store.start()
    loads[0].wait()
    small = small_ref[...]
    turned = small.T
    last = 64 + features_used
    pos_weight_out[...] = turned[64:last]
    pos_bias_out[...] = turned[last : last + 1]
    mid_bias_out[...] = turned[last + 1 : last + 2]
    mid_weight_out[...] = small[:, :64]
    for store in stores:
        store.wait()


def on_device(
    value_branch,
    first_gate,
    second_gate,
    out_cotangent,
    pos_weight,
    pos_bias,
    mid_weight,
    mid_bias,
    out_weight,
    decay_rates,
):
    model_width, tok_dev = value_branch.shape
    devices = lax.axis_size("seq")
    channels = model_width // devices
    hidden, features_used = pos_weight.shape
    fits = (
        tok_dev == RADIX
        and devices == 16
        and channels == 2 * GROUP
        and hidden == 64
        and features_used <= 61
        and out_weight.shape == (2 * model_width, 64)
    )
    if not fits:
        return on_device_plain(
            value_branch,
            first_gate,
            second_gate,
            out_cotangent,
            pos_weight,
            pos_bias,
            mid_weight,
            mid_bias,
            out_weight,
            decay_rates,
        )
    seq_len = tok_dev * devices
    freq_rows = 2 * devices
    tables = numpy_tables(freq_rows, RADIX, seq_len, (features_used - 1) // 2, GROUP)
    share = hidden // devices
    dma = pltpu.SemaphoreType.DMA
    vmem = pl.BlockSpec(memory_space=pltpu.VMEM)
    hbm = pl.BlockSpec(memory_space=pltpu.HBM)
    bf16, f32 = jnp.bfloat16, jnp.float32
    value_out, first_out, second_out, weight_out, small = pl.pallas_call(
        functools.partial(operator_kernel, devices, channels, features_used),
        out_shape=[jax.ShapeDtypeStruct((model_width, tok_dev), jnp.bfloat16)] * 3
        + [
            jax.ShapeDtypeStruct((2 * channels, hidden), jnp.float32),
            jax.ShapeDtypeStruct((devices, share, 2 * hidden), jnp.float32),
        ],
        in_specs=[hbm] * 17,
        out_specs=[vmem] * 5,
        scratch_shapes=[
            pltpu.VMEM((4, devices, channels, RADIX), jnp.bfloat16),
            pltpu.VMEM((3, devices, channels, RADIX), jnp.bfloat16),
            pltpu.VMEM((devices, share, 2 * hidden), jnp.float32),
            pltpu.VMEM((devices, share, 2 * hidden), jnp.float32),
            pltpu.VMEM((share, 2 * hidden), jnp.float32),
            dma((4, devices)),
            dma((4, devices)),
            dma((3, devices)),
            dma((3, devices)),
            dma((devices,)),
            dma((devices,)),
            dma((devices,)),
            dma((devices,)),
            pltpu.VMEM((features_used, hidden), f32),
            pltpu.VMEM((1, hidden), f32),
            pltpu.VMEM((hidden, hidden), f32),
            pltpu.VMEM((1, hidden), f32),
            pltpu.VMEM((hidden, 128), f32),
            pltpu.VMEM((2 * model_width // 128, 128), f32),
            *[pltpu.VMEM(table.shape, table.dtype) for table in tables],
            pltpu.VMEM((hidden, hidden), f32),
            dma((13,)),
            dma((4,)),
        ],
        compiler_params=pltpu.CompilerParams(
            collective_id=0, has_side_effects=True, vmem_limit_bytes=62 * 1024 * 1024
        ),
    )(
        value_branch,
        first_gate,
        second_gate,
        out_cotangent,
        pos_weight.T,
        pos_bias.reshape(1, hidden),
        mid_weight,
        mid_bias.reshape(1, hidden),
        out_weight.T,
        decay_rates.reshape(2 * model_width // 128, 128),
        *[jnp.asarray(table) for table in tables],
    )
    small = small.reshape(hidden, 2 * hidden)
    shape = jax.ShapeDtypeStruct
    results = pl.pallas_call(
        functools.partial(finish_kernel, features_used),
        out_shape=[shape((model_width, tok_dev), bf16)] * 3
        + [
            shape((2 * channels, hidden), f32),
            shape((features_used, hidden), f32),
            shape((1, hidden), f32),
            shape((hidden, hidden), f32),
            shape((1, hidden), f32),
        ],
        in_specs=[hbm] * 5,
        out_specs=[hbm] * 4 + [pl.BlockSpec()] * 4,
        scratch_shapes=[pltpu.VMEM((model_width, tok_dev), bf16)] * 3
        + [
            pltpu.VMEM((2 * channels, hidden), f32),
            pltpu.VMEM((hidden, 2 * hidden), f32),
            dma((5,)),
            dma((5,)),
        ],
        compiler_params=pltpu.CompilerParams(vmem_limit_bytes=62 * 1024 * 1024),
    )(value_out, first_out, second_out, weight_out, small)
    return (
        results[0],
        results[1],
        results[2],
        results[4].T,
        results[5].reshape(hidden),
        results[6],
        results[7].reshape(hidden),
        results[3],
    )


def solution(mesh):
    in_specs = (
        P(None, ("dp", "seq")),
        P(None, ("dp", "seq")),
        P(None, ("dp", "seq")),
        P(None, ("dp", "seq")),
        P(),
        P(),
        P(),
        P(),
        P(),
        P(),
    )
    out_specs = (
        P(None, ("dp", "seq")),
        P(None, ("dp", "seq")),
        P(None, ("dp", "seq")),
        P("dp", None),
        P("dp"),
        P("dp", None),
        P("dp"),
        P("seq", "dp"),
    )
    return jax.shard_map(
        on_device, mesh=mesh, in_specs=in_specs, out_specs=out_specs, check_vma=False
    )
```
